128 devices in a mesh: ctx: 16 (over z, x), pb: 8 (over y, core).
Axes of the slice: x: 4, y: 4, z: 4, core: 2. Of those that a mesh axis runs over, the one named last changes fastest.
Arguments:
- main_query: bfloat16 [512, 128, 576], P(('pb', 'ctx')), may hold values from -30 to 30
- main_key: bfloat16 [16384, 576], P('ctx'), may hold values from -4 to 4
- index_query: bfloat16 [512, 64, 128], P(('pb', 'ctx')), may hold values from -6 to 6
- index_key: bfloat16 [16384, 128], P('ctx'), may hold values from -0.36 to 0.36
- head_weight: bfloat16 [512, 64], P(('pb', 'ctx')), may hold values from -4 to 4
- query_positions: int32 [512], P('pb'), may hold values from 8192 to 16383
- key_positions: int32 [16384], replicated, may hold values from 0 to 16383, as said below
Outputs:
- divergence: float32 [], replicated
- grad_index_query: float32 [512, 64, 128], P(('pb', 'ctx'))
- grad_head_weight: float32 [512, 64], P(('pb', 'ctx'))
- grad_index_key: float32 [16384, 128], P(('ctx', 'pb'))
The draws below stay inside these ranges and needn't reach their ends.
Inputs may be any that keep to these rules, and one draw needn't show every extreme that they name: `key_positions`: each of 0 to 16383 once.
All inputs are finite; a program needn't handle non-finite values.
Results may differ from the reference program's by a relative error of at most 0.0018.
Values may be sent and summed in bfloat16 or wider, within the bound.
No kernel may reach another device: no remote copies, remote signals or barrier semaphores. Data moves between devices by JAX's collectives and lax.ppermute only.
A program may use at most 256 MiB of HBM per device.

```python
import jax
import jax.numpy as jnp
from jax import lax

H = 128
DR = 64
DN = 128
HI = 64
DI = 128
DK = 576
KEYS = 16384
QROWS = 512


def shared_draw(key):
    ordering = jax.random.permutation(jax.random.fold_in(key, 101), KEYS).astype(jnp.int32)
    chosen = jnp.argsort(ordering)[:2]
    sign_rows = jnp.where(jax.random.bernoulli(jax.random.fold_in(key, 102), 0.5, (2, DK)), 1.0, -1.0)
    index_signs = jnp.where(jax.random.bernoulli(jax.random.fold_in(key, 103), 0.5, (2, DI)), 1.0, -1.0)
    return (ordering, chosen, sign_rows, index_signs)


def peak_levels():
    return 120.0 + 36.0 * jnp.arange(8).astype(jnp.float32)


def draw_key_positions(key, part):
    ordering, chosen, sign_rows, index_signs = shared_draw(key)
    return ordering


def draw_main_key(key, part):
    ordering, chosen, sign_rows, index_signs = shared_draw(key)
    own_key = jax.random.fold_in(key, 3)
    key_values = jnp.clip(jax.random.normal(own_key, (KEYS, DK), jnp.float32), -4.0, 4.0)
    key_values = key_values.at[chosen[0]].set(4.0 * sign_rows[0]).at[chosen[1]].set(4.0 * sign_rows[1])
    return key_values.astype(jnp.bfloat16)


def draw_index_key(key, part):
    ordering, chosen, sign_rows, index_signs = shared_draw(key)
    own_key = jax.random.fold_in(key, 5)
    key_values = jnp.clip(jax.random.normal(own_key, (KEYS, DI), jnp.float32) * DI ** (-0.5), -0.35, 0.35)
    key_values = key_values.at[chosen[0]].set(0.35 * index_signs[0]).at[chosen[1]].set(0.35 * index_signs[1])
    return key_values.astype(jnp.bfloat16)


def draw_main_query(key, part):
    ordering, chosen, sign_rows, index_signs = shared_draw(key)
    own_key = jax.random.fold_in(key, 7)
    values = jnp.clip(jax.random.normal(own_key, (QROWS, H, DK), jnp.float32), -4.0, 4.0)
    aligned = sign_rows[0] + 0.9921875 * sign_rows[1]
    strengths = peak_levels() * (DN + DR) ** 0.5 / (4.0 * DK)
    aligned_rows = jnp.arange(8) * (QROWS // 8)
    values = values.at[aligned_rows].set(strengths[:, None, None] * aligned[None, None, :] + jnp.zeros((8, H, DK), jnp.float32))
    return values.astype(jnp.bfloat16)


def draw_index_query(key, part):
    ordering, chosen, sign_rows, index_signs = shared_draw(key)
    own_key = jax.random.fold_in(key, 9)
    values = jnp.clip(jax.random.normal(own_key, (QROWS, HI, DI), jnp.float32), -4.0, 4.0)
    aligned = index_signs[0] + 0.9921875 * index_signs[1]
    strengths = peak_levels() / (0.8 * 0.35 * HI * DI)
    aligned_rows = jnp.arange(8) * (QROWS // 8)
    values = values.at[aligned_rows].set(strengths[:, None, None] * aligned[None, None, :] + jnp.zeros((8, HI, DI), jnp.float32))
    return values.astype(jnp.bfloat16)


def draw_head_weight(key, part):
    own_key = jax.random.fold_in(key, 11)
    values = jnp.clip(jax.random.normal(own_key, (QROWS, HI), jnp.float32), -4.0, 4.0)
    aligned_rows = jnp.arange(8) * (QROWS // 8)
    values = values.at[aligned_rows].set(jnp.abs(values[aligned_rows]))
    return values.astype(jnp.bfloat16)


def set_ends(values, key, smallest, largest):
    place = [jax.random.randint(jax.random.fold_in(key, axis), (), 0, length) for axis, length in enumerate(values.shape)]
    widest = values.shape.index(max(values.shape))
    neighbour = place[:widest] + [(place[widest] + 1) % values.shape[widest]] + place[widest + 1:]
    return values.at[tuple(place)].set(smallest).at[tuple(neighbour)].set(largest)


def setup_inputs(seed: int = 0) -> dict:
    streams_of = jax.random.split(jax.random.key(seed), 8)
    main_query = draw_main_query(jax.random.fold_in(streams_of[7], 71), 0)
    main_key = draw_main_key(jax.random.fold_in(streams_of[7], 71), 0)
    index_query = draw_index_query(jax.random.fold_in(streams_of[7], 71), 0)
    index_key = draw_index_key(jax.random.fold_in(streams_of[7], 71), 0)
    head_weight = draw_head_weight(jax.random.fold_in(streams_of[7], 71), 0)
    query_positions = set_ends(jax.random.randint(streams_of[5], (QROWS,), KEYS // 2, KEYS), jax.random.fold_in(streams_of[5], 1), KEYS // 2, KEYS - 1).astype(jnp.int32)
    key_positions = draw_key_positions(jax.random.fold_in(streams_of[7], 71), 0)
    return dict(main_query=main_query, main_key=main_key, index_query=index_query, index_key=index_key, head_weight=head_weight, query_positions=query_positions, key_positions=key_positions)


NEGATIVE = -1e30


def reference(main_query, main_key, index_query, index_key, head_weight, query_positions, key_positions):
    score_scale = (DN + DR) ** -0.5
    row_block = 8
    block_count = QROWS // row_block
    inputs = (main_query.reshape(block_count, row_block, H, DK),
              index_query.reshape(block_count, row_block, HI, DI),
              head_weight.reshape(block_count, row_block, HI),
              query_positions.reshape(block_count, row_block))
    index_wide = index_key.astype(jnp.float32)

    def one_block(key_total, pieces):
        main_rows, index_rows, row_weights, row_positions = pieces
        visible = key_positions[None, :] <= row_positions[:, None]
        scores = jnp.dot(main_rows.reshape(row_block * H, DK), main_key.T, preferred_element_type=jnp.float32)
        scores = scores.reshape(row_block, H, KEYS) * score_scale
        scores = jnp.where(visible[:, None, :], scores, NEGATIVE)
        maxima = jnp.max(scores, -1)
        exp_terms = jnp.where(visible[:, None, :], jnp.exp(scores - maxima[:, :, None]), 0.0)
        totals = jnp.sum(exp_terms, -1)
        target = jnp.sum(exp_terms / totals[:, :, None], 1) / H
        flat_index = index_rows.reshape(row_block * HI, DI)
        products = jnp.dot(flat_index, index_key.T, preferred_element_type=jnp.float32).reshape(row_block, HI, KEYS)
        active = jnp.maximum(products, 0.0)
        weights_wide = row_weights.astype(jnp.float32)[:, :, None]
        logits = jnp.sum(weights_wide * active, 1)
        masked = jnp.where(visible, logits, NEGATIVE)
        index_maxima = jnp.max(masked, -1)
        index_exp = jnp.where(visible, jnp.exp(masked - index_maxima[:, None]), 0.0)
        index_totals = jnp.sum(index_exp, -1)
        prob = index_exp / index_totals[:, None]
        log_norm = index_maxima + jnp.log(index_totals)
        loss_rows = jnp.sum(jnp.where(visible, jax.scipy.special.xlogy(target, target) - target * (logits - log_norm[:, None]), 0.0), -1)
        deltas = prob - target
        grad_weight = jnp.sum(deltas[:, None, :] * active, -1)
        pulled = jnp.where(products > 0, deltas[:, None, :] * weights_wide, 0.0)
        pulled = pulled.reshape(row_block * HI, KEYS)
        grad_query = jnp.dot(pulled, index_wide, preferred_element_type=jnp.float32,
                             precision=lax.Precision.HIGHEST).reshape(row_block, HI, DI)
        key_total = key_total + jnp.dot(pulled.T, flat_index.astype(jnp.float32), preferred_element_type=jnp.float32,
                                        precision=lax.Precision.HIGHEST)
        return key_total, (loss_rows, grad_query, grad_weight)

    key_total, outputs = lax.scan(one_block, jnp.zeros((KEYS, DI), jnp.float32), inputs)
    loss_rows, grad_query, grad_weight = outputs
    divergence = jnp.sum(loss_rows) / QROWS
    return (divergence, grad_query.reshape(QROWS, HI, DI), grad_weight.reshape(QROWS, HI), key_total)
```

```python
import jax
import jax.numpy as jnp
from jax import lax
from jax.experimental import pallas as pl
from jax.experimental.pallas import tpu as pltpu
from jax.sharding import Mesh, PartitionSpec as P

H = 128
DR = 64
DN = 128
HI = 64
DI = 128
DK = 576
ROWS = 4
SLOTS = 4
GROUP = ROWS * SLOTS
SHARD = 1024
HALF = SHARD // 2
PACK = ROWS * HI + 16
ROW_TOTAL = 512
NEGATIVE = -1e30
LOG2E = 1.4426950408889634
SCALE2 = (DN + DR) ** (-0.5) * LOG2E
F32 = jnp.float32
BF16 = jnp.bfloat16
VMEM_LIMIT = 56 * 1024 * 1024


def whole(shape):
    return pl.BlockSpec(shape, lambda *_: (0,) * len(shape))


def smem():
    return pl.BlockSpec(memory_space=pltpu.SMEM)


def vmem():
    return pl.BlockSpec(memory_space=pltpu.VMEM)


def params():
    return pltpu.CompilerParams(vmem_limit_bytes=VMEM_LIMIT)


def cost(flops, byte_count, transcendentals=0):
    return pl.CostEstimate(flops=flops, bytes_accessed=byte_count, transcendentals=transcendentals)


def contract(a, b, dim_a, dim_b):
    return lax.dot_general(a, b, (((dim_a,), (dim_b,)), ((), ())), preferred_element_type=F32)


def row_position(place, qpos, slot, row):
    return qpos[place[0] * GROUP + lax.rem(place[1] + slot, SLOTS) * ROWS + row]


def index_kernel(place, qpos, kpos, *refs):
    packs, halves = refs[:SLOTS], refs[SLOTS : 3 * SLOTS]
    logits, places, stats, scores = refs[3 * SLOTS :]
    z, x, core = place[0], place[1], place[2]
    weights = [packs[slot][ROWS * HI :, :].astype(F32).T for slot in range(SLOTS)]
    for step in range(SLOTS):
        base = (lax.rem(z + step, SLOTS) * SLOTS + x) * 8
        pieces = [kpos[pl.ds(base + 2 * y + core, 1), :] for y in range(4)]
        pieces += [kpos[pl.ds(base + 2 * y + 1 - core, 1), :] for y in range(4)]
        position = jnp.concatenate(pieces, axis=1)
        places[step] = jnp.broadcast_to(position, (8, SHARD))
        columns = slice(step * SHARD, (step + 1) * SHARD)
        for slot in range(SLOTS):
            queries = packs[slot][: ROWS * HI, :]
            for side in range(2):
                scores[:, side * HALF : (side + 1) * HALF] = contract(
                    queries, halves[2 * step + side][...], 1, 1
                )
            for row in range(ROWS):
                active = jnp.maximum(scores[row * HI : (row + 1) * HI, :], 0.0)
                line = jnp.sum(active * weights[slot][:HI, row : row + 1], axis=0, keepdims=True)
                visible = position <= row_position(place, qpos, slot, row)
                at = slot * ROWS + row
                logits[at : at + 1, columns] = jnp.where(visible, line, NEGATIVE)
    values = logits[...]
    best = jnp.max(values, axis=1, keepdims=True)
    total = jnp.sum(jnp.exp2((values - best) * LOG2E), axis=1, keepdims=True)
    stats[:GROUP, :] = jnp.broadcast_to(best, (GROUP, 128))
    stats[GROUP:, :] = jnp.broadcast_to(total, (GROUP, 128))


def index_pass(place, qpos, kpos, packs, key_halves):
    return pl.pallas_call(
        index_kernel,
        in_specs=[smem(), smem()] + [vmem()] * (1 + 3 * SLOTS),
        out_specs=[vmem()] * 3,
        out_shape=(
            jax.ShapeDtypeStruct((GROUP, SLOTS * SHARD), F32),
            jax.ShapeDtypeStruct((SLOTS, 8, SHARD), jnp.int32),
            jax.ShapeDtypeStruct((2 * GROUP, 128), F32),
        ),
        scratch_shapes=[pltpu.VMEM((ROWS * HI, SHARD), F32)],
        compiler_params=params(),
        cost_estimate=cost(2 * GROUP * HI * DI * SLOTS * SHARD * 4, 2000000),
        name="index_pass",
    )(place, qpos, kpos, *packs, *key_halves)


def score_kernel(step, place, qpos, places, *refs):
    queries, halves = refs[:SLOTS], refs[SLOTS : SLOTS + 2]
    terms, stats, turned, scores = refs[SLOTS + 2 :]
    slot = pl.program_id(0)
    for index in range(SLOTS):

        @pl.when(slot == index)
        def _():
            for row in range(ROWS):
                turned[row * H : (row + 1) * H, :] = queries[index][row].T

    for side in range(2):
        scores[:, side * HALF : (side + 1) * HALF] = contract(turned[...], halves[side][...], 1, 0)
    position = places[step, 0:1, :]
    lane = lax.broadcasted_iota(jnp.int32, (H, 128), 1)
    kept = jnp.where(slot == 0, jnp.zeros((H, 128), F32), stats[...])
    for row in range(ROWS):
        visible = position <= row_position(place, qpos, slot, row)
        values = jnp.where(visible, scores[row * H : (row + 1) * H, :], NEGATIVE)
        best = jnp.max(values, axis=1, keepdims=True)
        part = jnp.exp2((values - best) * SCALE2)
        total = jnp.sum(part, axis=1, keepdims=True)
        terms[row] = part
        at = slot * ROWS + row
        kept = jnp.where(lane == at, best, jnp.where(lane == GROUP + at, total, kept))
    stats[...] = kept


def score_pass(step, place, qpos, places, queries, halves):
    return pl.pallas_call(
        lambda *refs: score_kernel(step, *refs),
        grid=(SLOTS,),
        in_specs=[smem(), smem(), whole((SLOTS, 8, SHARD))]
        + [whole((ROWS, DK, H))] * SLOTS
        + [whole((DK, HALF))] * 2,
        out_specs=[
            pl.BlockSpec((ROWS, H, SHARD), lambda i: (i, 0, 0)),
            whole((H, 128)),
        ],
        out_shape=(
            jax.ShapeDtypeStruct((GROUP, H, SHARD), F32),
            jax.ShapeDtypeStruct((H, 128), F32),
        ),
        scratch_shapes=[pltpu.VMEM((ROWS * H, DK), BF16), pltpu.VMEM((ROWS * H, SHARD), F32)],
        compiler_params=params(),
        cost_estimate=cost(2 * GROUP * H * DK * SHARD, 12000000, GROUP * H * SHARD),
        name="score_pass",
    )(place, qpos, places, *queries, *halves)


def combine_kernel(*refs):
    parts, index_stats, message = refs[:SLOTS], refs[SLOTS], refs[SLOTS + 1]
    lane = lax.broadcasted_iota(jnp.int32, (H, 128), 1)
    values = [part[...] for part in parts]
    best = largest(values)
    total = jnp.zeros((H, 128), F32)
    for value in values:
        factor = pltpu.roll(jnp.exp2((value - best) * SCALE2), GROUP, 1)
        total = total + value * jnp.where((lane >= GROUP) & (lane < 2 * GROUP), factor, 0.0)
    both = jnp.where(lane < GROUP, best, total)
    message[: 2 * GROUP, :] = both.T[: 2 * GROUP, :]
    message[2 * GROUP :, :] = index_stats[...]


def largest(values):
    best = values[0]
    for value in values[1:]:
        best = jnp.maximum(best, value)
    return best


def combine_pass(parts, index_stats):
    return pl.pallas_call(
        combine_kernel,
        in_specs=[vmem()] * (SLOTS + 1),
        out_specs=vmem(),
        out_shape=jax.ShapeDtypeStruct((4 * GROUP, 128), F32),
        compiler_params=params(),
        cost_estimate=cost(1000000, 400000),
        name="combine_pass",
    )(*parts, index_stats)


def target_kernel(*refs):
    messages, parts, logits = refs[:SLOTS], refs[SLOTS : 2 * SLOTS], refs[2 * SLOTS]

    def field(index):
        return [
            jnp.concatenate(
                [
                    message[pl.ds(index * GROUP + (i - k) % SLOTS * ROWS, ROWS), :]
                    for i in range(SLOTS)
                ],
                axis=0,
            )
            for k, message in enumerate(messages)
        ]

    terms = refs[2 * SLOTS + 1 : 3 * SLOTS + 1]
    deltas, loss, factors, target = refs[3 * SLOTS + 1 :]
    slot = pl.program_id(0)

    @pl.when(slot == 0)
    def _():
        maxima, totals = field(0), field(1)
        best = largest(maxima)
        total = jnp.zeros((GROUP, 128), F32)
        for k in range(SLOTS):
            total = total + totals[k] * jnp.exp2((maxima[k] - best) * SCALE2)
        both = jnp.concatenate([best, 1.0 / (total * H), jnp.zeros((96, 128), F32)], axis=0).T
        for step in range(SLOTS):
            factor = (
                jnp.exp2((parts[step][:, :GROUP] - both[:, :GROUP]) * SCALE2)
                * both[:, GROUP : 2 * GROUP]
            )
            for index in range(SLOTS):
                factors[index, :, step * ROWS : (step + 1) * ROWS] = factor[
                    :, index * ROWS : (index + 1) * ROWS
                ]

    mine = factors[slot]
    for step in range(SLOTS):
        columns = slice(step * SHARD, (step + 1) * SHARD)
        lines = []
        for row in range(ROWS):
            at = step * ROWS + row
            lines.append(jnp.sum(terms[step][row] * mine[:, at : at + 1], axis=0, keepdims=True))
        target[slot, :, columns] = jnp.concatenate(lines + lines, axis=0)

    @pl.when(slot == SLOTS - 1)
    def _():
        maxima, totals = field(2), field(3)
        best = largest(maxima)
        total = jnp.zeros((GROUP, 128), F32)
        for k in range(SLOTS):
            total = total + totals[k] * jnp.exp2((maxima[k] - best) * LOG2E)
        best, total = best[:, :1], total[:, :1]
        norm = best + jnp.log(total)
        share = 1.0 / total
        lost = jnp.zeros((GROUP, 1), F32)
        for step in range(SLOTS):
            columns = slice(step * SHARD, (step + 1) * SHARD)
            wanted = jnp.concatenate([target[i, :ROWS, columns] for i in range(SLOTS)], axis=0)
            value = logits[:, columns]
            prob = jnp.exp2((value - best) * LOG2E) * share
            deltas[:, columns] = prob - wanted
            pieces = wanted * (jnp.log(jnp.maximum(wanted, 1e-37)) - (value - norm))
            lost = lost + jnp.sum(jnp.where(wanted > 0, pieces, 0.0), axis=1, keepdims=True)
        loss[...] = jnp.broadcast_to(jnp.sum(lost, axis=0, keepdims=True), (8, 128))


def target_pass(messages, parts, logits, terms):
    return pl.pallas_call(
        target_kernel,
        grid=(SLOTS,),
        in_specs=[whole((4 * GROUP, 128))] * SLOTS
        + [whole((H, 128))] * SLOTS
        + [whole((GROUP, SLOTS * SHARD))]
        + [pl.BlockSpec((ROWS, H, SHARD), lambda i: (i, 0, 0))] * SLOTS,
        out_specs=[whole((GROUP, SLOTS * SHARD)), whole((8, 128))],
        out_shape=(
            jax.ShapeDtypeStruct((GROUP, SLOTS * SHARD), F32),
            jax.ShapeDtypeStruct((8, 128), F32),
        ),
        scratch_shapes=[
            pltpu.VMEM((SLOTS, H, GROUP), F32),
            pltpu.VMEM((SLOTS, 8, SLOTS * SHARD), F32),
        ],
        compiler_params=params(),
        cost_estimate=cost(2 * GROUP * H * SLOTS * SHARD, 34000000),
        name="target_pass",
    )(*messages, *parts, logits, *terms)


def gradient_kernel(*refs):
    deltas, packs, halves = refs[0], refs[1 : SLOTS + 1], refs[SLOTS + 1 : SLOTS + 3]
    before = refs[SLOTS + 3]
    key_near, key_far, query_grad, highs, lows = refs[SLOTS + 4 :]
    total = [jnp.zeros((2 * DI, HALF), F32), jnp.zeros((2 * DI, HALF), F32)]
    for slot in range(SLOTS):
        queries = packs[slot][: ROWS * HI, :]
        weights = packs[slot][ROWS * HI :, :].astype(F32).T
        product = jnp.concatenate(
            [
                queries[row * HI : (row + 1) * HI].astype(F32) * weights[:HI, row : row + 1]
                for row in range(ROWS)
            ],
            axis=0,
        )
        high = product.astype(BF16).astype(F32)
        both = jnp.concatenate([high.T, (product - high).T], axis=0).astype(BF16)
        part = slice(slot * ROWS * HI, (slot + 1) * ROWS * HI)
        gained = before[part, :]
        for side in range(2):
            keys = halves[side][...]
            scores = contract(queries, keys, 1, 1)
            for row in range(ROWS):
                at = slot * ROWS + row
                delta = deltas[at : at + 1, side * HALF : (side + 1) * HALF]
                delta_high = delta.astype(BF16).astype(F32)
                delta_low = delta - delta_high
                active = scores[row * HI : (row + 1) * HI, :] > 0
                highs[row * HI : (row + 1) * HI, :] = jnp.where(active, delta_high, 0.0).astype(BF16)
                lows[row * HI : (row + 1) * HI, :] = jnp.where(active, delta_low, 0.0).astype(BF16)
            masked_high, masked_low = highs[...], lows[...]
            gained = gained + contract(masked_high, keys, 1, 0) + contract(masked_low, keys, 1, 0)
            wide = contract(both, masked_high, 1, 0)
            narrow = contract(both[:DI], masked_low, 1, 0)
            total[side] = total[side] + jnp.concatenate([wide[:DI] + narrow, wide[DI:]], axis=0)
        query_grad[part, :] = gained
    key_near[...] = total[0][:DI] + total[0][DI:]
    key_far[...] = total[1][:DI] + total[1][DI:]


def gradient_pass(step, deltas, packs, halves, before):
    return pl.pallas_call(
        gradient_kernel,
        grid=(1,),
        in_specs=[pl.BlockSpec((GROUP, SHARD), lambda i: (0, step))]
        + [whole((PACK, DI))] * SLOTS
        + [whole((HALF, DI))] * 2
        + [whole((GROUP * HI, DI))],
        out_specs=[whole((DI, HALF))] * 2 + [whole((GROUP * HI, DI))],
        out_shape=(
            jax.ShapeDtypeStruct((DI, HALF), F32),
            jax.ShapeDtypeStruct((DI, HALF), F32),
            jax.ShapeDtypeStruct((GROUP * HI, DI), F32),
        ),
        scratch_shapes=[pltpu.VMEM((ROWS * HI, HALF), BF16)] * 2,
        compiler_params=params(),
        cost_estimate=cost(2 * GROUP * HI * DI * SHARD * 8, 4000000),
        name="gradient_pass",
    )(deltas, *packs, *halves, before)


def pulled_from(value, axis, offset):
    size = lax.axis_size(axis)
    return lax.ppermute(value, axis, [((i + offset) % size, i) for i in range(size)])


def around(value, axis):
    return [value] + [pulled_from(value, axis, k) for k in range(1, lax.axis_size(axis))]


def local(
    main_query, main_key, index_query, index_key, head_weight, query_positions, key_positions
):
    z, x, y, core = (lax.axis_index(name) for name in ("z", "x", "y", "c"))
    place = jnp.stack([z, x, core, y]).astype(jnp.int32)
    kpos = key_positions.reshape(128, 128)

    weights = jnp.pad(head_weight, ((0, 12), (0, DI - HI)))
    pack = jnp.concatenate([index_query.reshape(ROWS * HI, DI), weights], axis=0)
    split = index_key.reshape(4, 2, 128, DI)
    near = jnp.where(core == 0, split[:, 0], split[:, 1]).reshape(HALF, DI)
    far = jnp.where(core == 0, split[:, 1], split[:, 0]).reshape(HALF, DI)
    packs = around(pack, "x")
    index_near = around(near, "z")
    index_far = [far] + [pulled_from(value, "c", 1) for value in index_near[1:]]

    turned = main_query.transpose(0, 2, 1)
    queries = around(turned, "x")
    split = main_key.T.reshape(DK, 4, 2, 128)
    near = jnp.where(core == 0, split[:, :, 0], split[:, :, 1]).reshape(DK, HALF)
    far = jnp.where(core == 0, split[:, :, 1], split[:, :, 0]).reshape(DK, HALF)
    main_near = around(near, "z")
    main_far = [far] + [pulled_from(value, "c", 1) for value in main_near[1:]]

    index_halves = [half for pair in zip(index_near, index_far) for half in pair]
    logits, places, index_stats = index_pass(place, query_positions, kpos, packs, index_halves)

    order = (0, 1, 3, 2)
    terms, parts = [None] * SLOTS, [None] * SLOTS
    for step in order:
        terms[step], parts[step] = score_pass(
            step, place, query_positions, places, queries, (main_near[step], main_far[step])
        )
    message = combine_pass(parts, index_stats)
    messages = around(message, "x")
    deltas, loss = target_pass(messages, parts, logits, terms)

    loss = sum(around(loss, "x"))
    loss = sum(around(loss, "z"))
    loss = sum(around(loss, "y"))
    loss = sum(around(loss, "c"))
    divergence = loss[0, 0] / ROW_TOTAL

    query_grad = jnp.zeros((GROUP * HI, DI), F32)
    key_parts = []
    for step in (2, 1, 3, 0):
        key_near, key_far, query_grad = gradient_pass(
            step, deltas, packs, (index_near[step], index_far[step]), query_grad
        )
        mine = key_near + pulled_from(key_far, "c", 1)
        key_parts.append(pulled_from(mine, "z", -step) if step else mine)
    key_sum = sum(key_parts)
    blocks = [
        lax.dynamic_slice_in_dim(key_sum, lax.rem(y + k, 4) * 128, 128, 1) for k in range(4)
    ]
    key_total = blocks[0]
    for k in range(1, 4):
        key_total = key_total + pulled_from(blocks[k], "y", -k)

    rows = query_grad.reshape(SLOTS, ROWS * HI, DI)
    row_total = rows[0]
    for k in range(1, SLOTS):
        row_total = row_total + pulled_from(rows[k], "x", -k)
    row_total = row_total.reshape(ROWS, HI, DI)
    grad_query = row_total * head_weight.astype(F32)[:, :, None]
    grad_weight = jnp.sum(row_total * index_query.astype(F32), axis=-1)
    return (divergence, grad_query, grad_weight, key_total.T)


def solution(mesh):
    fine = Mesh(mesh.devices.reshape(4, 4, 4, 2), ("z", "x", "y", "c"))
    rows = ("y", "c", "z", "x")
    keys = ("z", "x")
    return jax.shard_map(
        local,
        mesh=fine,
        in_specs=(
            P(rows, None, None),
            P(keys, None),
            P(rows, None, None),
            P(keys, None),
            P(rows, None),
            P(("y", "c")),
            P(),
        ),
        out_specs=(
            P(),
            P(rows, None, None),
            P(rows, None),
            P(("z", "x", "y", "c"), None),
        ),
        check_vma=False,
    )
```

```python
import jax
import jax.numpy as jnp
from jax import lax
from jax.experimental import pallas as pl
from jax.experimental.pallas import tpu as pltpu
from jax.sharding import Mesh, PartitionSpec as P

H = 128
DR = 64
DN = 128
HI = 64
DI = 128
DK = 576
ROWS = 4
SLOTS = 4
GROUP = ROWS * SLOTS
SHARD = 1024
HALF = SHARD // 2
DEEP = DK + GROUP
PACK = ROWS * HI + 16
LOW_ROWS = 2 * DK
HIGH_ROWS = 2 * DK + PACK
CUT = (DK + DI) // 2
ROW_TOTAL = 512
NEGATIVE = -1e30
LOG2E = 1.4426950408889634
SCALE2 = (DN + DR) ** (-0.5) * LOG2E
F32 = jnp.float32
BF16 = jnp.bfloat16
VMEM_LIMIT = 12 * 1024 * 1024
NEAR = (0, 1, 3)
ALL = (0, 1, 2, 3)
FIRST = [(step, slot) for step in NEAR for slot in NEAR]
LAST = [(step, 2) for step in NEAR] + [(2, slot) for slot in ALL]


def call(kernel, inputs, outputs, scratch=(), name=None, flops=0, moved=0, exps=0):
    return pl.pallas_call(
        kernel,
        in_specs=[
            pl.BlockSpec(memory_space=pltpu.SMEM if value.ndim == 1 else pltpu.VMEM)
            for value in inputs
        ],
        out_specs=[pl.BlockSpec(memory_space=pltpu.VMEM)] * len(outputs),
        out_shape=[jax.ShapeDtypeStruct(shape, dtype) for shape, dtype in outputs],
        scratch_shapes=[pltpu.VMEM(shape, dtype) for shape, dtype in scratch],
        compiler_params=pltpu.CompilerParams(vmem_limit_bytes=VMEM_LIMIT),
        cost_estimate=pl.CostEstimate(flops=flops, bytes_accessed=moved, transcendentals=exps),
        name=name,
    )(*inputs)


def contract(a, b, dim_a, dim_b):
    return lax.dot_general(a, b, (((dim_a,), (dim_b,)), ((), ())), preferred_element_type=F32)


def largest(values):
    best = values[0]
    for value in values[1:]:
        best = jnp.maximum(best, value)
    return best


def row_position(place, qpos, slot, row):
    return qpos[place[0] * GROUP + lax.rem(place[1] + slot, SLOTS) * ROWS + row]


def key_positions_of(place, kpos, step):
    core = place[2]
    base = (lax.rem(place[0] + step, SLOTS) * SLOTS + place[1]) * 8
    pieces = [kpos[pl.ds(base + 2 * y + core, 1), :] for y in range(4)]
    pieces += [kpos[pl.ds(base + 2 * y + 1 - core, 1), :] for y in range(4)]
    return jnp.concatenate(pieces, axis=1)


def row_prep_kernel(query, index_query, weight, low, high):
    for row in range(2):
        low[row * DK : (row + 1) * DK, :] = query[row]
        high[row * DK : (row + 1) * DK, :] = query[row + 2]
    high[LOW_ROWS : LOW_ROWS + ROWS * HI, :] = index_query[...]
    high[LOW_ROWS + ROWS * HI :, :] = weight[...]


def key_prep_kernel(place, main_key, index_key, near_low, near_high, far_low, far_high):
    core = place[2]
    turned = index_key[...].T
    for y in range(4):
        at = slice(y * 128, (y + 1) * 128)
        even = slice(2 * y * 128, (2 * y + 1) * 128)
        odd = slice((2 * y + 1) * 128, (2 * y + 2) * 128)
        for own, low, high in ((0, near_low, near_high), (1, far_low, far_high)):
            pick = jnp.broadcast_to(core == own, (1, 128))
            low[:, at] = jnp.where(pick, main_key[:CUT, even], main_key[:CUT, odd])
            high[: DK - CUT, at] = jnp.where(pick, main_key[CUT:, even], main_key[CUT:, odd])
            high[DK - CUT :, at] = jnp.where(pick, turned[:, even], turned[:, odd])


def turn_kernel(slot, low, high, turned):
    lane = lax.broadcasted_iota(jnp.int32, (H, GROUP), 1)
    for row in range(ROWS):
        source = low if row < 2 else high
        part = slice(row * H, (row + 1) * H)
        turned[part, :DK] = source[row % 2 * DK : (row % 2 + 1) * DK, :].T
        turned[part, DK:] = jnp.where(lane == slot * ROWS + row, 1.0, 0.0).astype(BF16)


def turn(slot, low, high):
    return call(
        lambda *refs: turn_kernel(slot, *refs),
        [low, high],
        [((ROWS * H, DEEP), BF16)],
        name="turn",
        moved=1300000,
    )[0]


def index_units(units, place, qpos, kpos, packs, keys, logits, scores):
    weights = {}
    for step, slot in units:
        position = key_positions_of(place, kpos, step)
        if slot not in weights:
            weights[slot] = packs[slot][LOW_ROWS + ROWS * HI :, :].astype(F32).T
        queries = packs[slot][LOW_ROWS : LOW_ROWS + ROWS * HI, :]
        for side in range(2):
            scores[:, side * HALF : (side + 1) * HALF] = contract(
                queries, keys[step][side][DK - CUT :, :], 1, 0
            )
        for row in range(ROWS):
            active = jnp.maximum(scores[row * HI : (row + 1) * HI, :], 0.0)
            line = jnp.sum(active * weights[slot][:HI, row : row + 1], axis=0, keepdims=True)
            visible = position <= row_position(place, qpos, slot, row)
            at = slot * ROWS + row
            logits[at : at + 1, step * SHARD : (step + 1) * SHARD] = jnp.where(
                visible, line, NEGATIVE
            )


def index_first_kernel(place, qpos, kpos, *refs):
    packs = dict(zip(NEAR, refs[:3]))
    keys = {step: refs[3 + 2 * i : 5 + 2 * i] for i, step in enumerate(NEAR)}
    logits, scores = refs[9:]
    logits[...] = jnp.zeros(logits.shape, F32)
    index_units(FIRST, place, qpos, kpos, packs, keys, logits, scores)


def index_last_kernel(place, qpos, kpos, before, *refs):
    packs = dict(zip(ALL, refs[:4]))
    keys = {step: refs[4 + 2 * step : 6 + 2 * step] for step in ALL}
    logits, stats, scores = refs[12:]
    logits[...] = before[...]
    index_units(LAST, place, qpos, kpos, packs, keys, logits, scores)
    values = logits[...]
    best = jnp.max(values, axis=1, keepdims=True)
    total = jnp.sum(jnp.exp2((values - best) * LOG2E), axis=1, keepdims=True)
    stats[:GROUP, :] = jnp.broadcast_to(best, (GROUP, 128))
    stats[GROUP:, :] = jnp.broadcast_to(total, (GROUP, 128))


def score_units(units, place, qpos, kpos, queries, key_parts, terms, stats, keys):
    lane = lax.broadcasted_iota(jnp.int32, (H, 128), 1)
    staged = None
    waiting = []

    def finish(unit, pair, at):
        step, slot = units[unit]
        for row in range(2 * pair, 2 * pair + 2):
            values = terms[unit * ROWS + row]
            best = jnp.max(values, axis=1, keepdims=True)
            part = jnp.exp2((values - best) * SCALE2)
            total = jnp.sum(part, axis=1, keepdims=True)
            terms[unit * ROWS + row] = part
            index = slot * ROWS + row
            stats[step] = jnp.where(
                lane == index, best, jnp.where(lane == GROUP + index, total, stats[step])
            )

    for unit, (step, slot) in enumerate(units):
        if staged != step:
            staged = step
            low_near, high_near, low_far, high_far = key_parts[step]
            for side, (low, high) in enumerate(((low_near, high_near), (low_far, high_far))):
                part = slice(side * HALF, (side + 1) * HALF)
                keys[:CUT, part] = low[...]
                keys[CUT:DK, part] = high[: DK - CUT, :]
            position = key_positions_of(place, kpos, step)
            hidden = [
                jnp.where(position <= row_position(place, qpos, i // ROWS, i % ROWS), 0.0, NEGATIVE)
                for i in range(GROUP)
            ]
            keys[DK:, :] = jnp.concatenate(hidden, axis=0).astype(BF16)
        for pair in range(2):
            part = slice(2 * pair * H, (2 * pair + 2) * H)
            start = unit * ROWS + 2 * pair
            product = contract(queries[slot][part, :], keys[...], 1, 0)
            terms[start : start + 2] = product.reshape(2, H, SHARD)
            if waiting:
                finish(*waiting.pop())
            waiting.append((unit, pair, start))
    finish(*waiting.pop())


def score_first_kernel(place, qpos, kpos, *refs):
    queries = dict(zip(NEAR, refs[:3]))
    key_parts = {step: refs[3 + 4 * i : 7 + 4 * i] for i, step in enumerate(NEAR)}
    terms, stat_out, keys = refs[15:]
    stats = {step: jnp.zeros((H, 128), F32) for step in NEAR}
    score_units(FIRST, place, qpos, kpos, queries, key_parts, terms, stats, keys)
    for step in NEAR:
        stat_out[step] = stats[step]
    stat_out[2] = jnp.zeros((H, 128), F32)


def score_last_kernel(place, qpos, kpos, before, index_stats, *refs):
    queries = dict(zip(ALL, refs[:4]))
    key_parts = {step: refs[4 + 4 * step : 8 + 4 * step] for step in ALL}
    terms, stat_out, message, keys = refs[20:]
    stats = {step: before[step] for step in ALL}
    score_units(LAST, place, qpos, kpos, queries, key_parts, terms, stats, keys)
    lane = lax.broadcasted_iota(jnp.int32, (H, 128), 1)
    best = largest([stats[step] for step in ALL])
    total = jnp.zeros((H, 128), F32)
    for step in ALL:
        stat_out[step] = stats[step]
        factor = pltpu.roll(jnp.exp2((stats[step] - best) * SCALE2), GROUP, 1)
        total = total + stats[step] * jnp.where(
            (lane >= GROUP) & (lane < 2 * GROUP), factor, 0.0
        )
    both = jnp.where(lane < GROUP, best, total)
    message[: 2 * GROUP, :] = both.T[: 2 * GROUP, :]
    message[2 * GROUP :, :] = index_stats[...]


def target_kernel(*refs):
    messages, stats, logits, first, last = refs[:4], refs[4], refs[5], refs[6], refs[7]
    deltas, loss, target = refs[8:]

    def field(index):
        return [
            jnp.concatenate(
                [
                    message[pl.ds(index * GROUP + (i - k) % SLOTS * ROWS, ROWS), :]
                    for i in range(SLOTS)
                ],
                axis=0,
            )
            for k, message in enumerate(messages)
        ]

    maxima, totals = field(0), field(1)
    best = largest(maxima)
    total = jnp.zeros((GROUP, 128), F32)
    for k in range(SLOTS):
        total = total + totals[k] * jnp.exp2((maxima[k] - best) * SCALE2)
    both = jnp.concatenate([best, 1.0 / (total * H), jnp.zeros((96, 128), F32)], axis=0).T
    factors = [
        jnp.exp2((stats[step][:, :GROUP] - both[:, :GROUP]) * SCALE2) * both[:, GROUP : 2 * GROUP]
        for step in ALL
    ]
    for terms, units in ((first, FIRST), (last, LAST)):
        for unit, (step, slot) in enumerate(units):
            for row in range(ROWS):
                at = slot * ROWS + row
                target[at : at + 1, step * SHARD : (step + 1) * SHARD] = jnp.sum(
                    terms[unit * ROWS + row] * factors[step][:, at : at + 1],
                    axis=0,
                    keepdims=True,
                )
    maxima, totals = field(2), field(3)
    best = largest(maxima)
    total = jnp.zeros((GROUP, 128), F32)
    for k in range(SLOTS):
        total = total + totals[k] * jnp.exp2((maxima[k] - best) * LOG2E)
    best, total = best[:, :1], total[:, :1]
    norm = best + jnp.log(total)
    share = 1.0 / total
    lost = jnp.zeros((GROUP, 1), F32)
    for step in range(SLOTS):
        columns = slice(step * SHARD, (step + 1) * SHARD)
        wanted = target[:, columns]
        value = logits[:, columns]
        prob = jnp.exp2((value - best) * LOG2E) * share
        deltas[:, columns] = prob - wanted
        pieces = wanted * (jnp.log(jnp.maximum(wanted, 1e-37)) - (value - norm))
        lost = lost + jnp.sum(jnp.where(wanted > 0, pieces, 0.0), axis=1, keepdims=True)
    loss[...] = jnp.broadcast_to(jnp.sum(lost, axis=0, keepdims=True), (8, 128))


def gradient_kernel(step, deltas, before, *refs):
    packs, halves = refs[:SLOTS], refs[SLOTS : SLOTS + 2]
    key_near, key_far = refs[SLOTS + 2 : SLOTS + 4]
    query_grads, highs, lows = refs[SLOTS + 4 : -2], refs[-2], refs[-1]
    total = [jnp.zeros((2 * DI, HALF), F32), jnp.zeros((2 * DI, HALF), F32)]
    for slot in range(SLOTS):
        queries = packs[slot][LOW_ROWS : LOW_ROWS + ROWS * HI, :]
        weights = packs[slot][LOW_ROWS + ROWS * HI :, :].astype(F32).T
        product = jnp.concatenate(
            [
                queries[row * HI : (row + 1) * HI].astype(F32) * weights[:HI, row : row + 1]
                for row in range(ROWS)
            ],
            axis=0,
        )
        high = product.astype(BF16).astype(F32)
        both = jnp.concatenate([high.T, (product - high).T], axis=0).astype(BF16)
        part = slice(slot * ROWS * HI, (slot + 1) * ROWS * HI)
        gained = before[part, :] if before is not None else None
        for side in range(2):
            keys = halves[side][DK - CUT :, :]
            scores = contract(queries, keys, 1, 0)
            for row in range(ROWS):
                at = slot * ROWS + row
                start = step * SHARD + side * HALF
                delta = deltas[at : at + 1, start : start + HALF]
                delta_high = delta.astype(BF16).astype(F32)
                delta_low = delta - delta_high
                active = scores[row * HI : (row + 1) * HI, :] > 0
                highs[row * HI : (row + 1) * HI, :] = jnp.where(active, delta_high, 0.0).astype(BF16)
                lows[row * HI : (row + 1) * HI, :] = jnp.where(active, delta_low, 0.0).astype(BF16)
            masked_high, masked_low = highs[...], lows[...]
            more = contract(masked_high, keys, 1, 1) + contract(masked_low, keys, 1, 1)
            gained = more if gained is None else gained + more
            wide = contract(both, masked_high, 1, 0)
            narrow = contract(both[:DI], masked_low, 1, 0)
            total[side] = total[side] + jnp.concatenate([wide[:DI] + narrow, wide[DI:]], axis=0)
        if len(query_grads) == 1:
            query_grads[0][part, :] = gained
        else:
            query_grads[slot][...] = gained
    key_near[...] = total[0][:DI] + total[0][DI:]
    key_far[...] = total[1][:DI] + total[1][DI:]


def gradient_pass(step, deltas, before, packs, halves, final):
    if before is None:
        kernel = lambda deltas, *refs: gradient_kernel(step, deltas, None, *refs)
        inputs = [deltas, *packs, *halves]
    else:
        kernel = lambda *refs: gradient_kernel(step, *refs)
        inputs = [deltas, before, *packs, *halves]
    if final:
        grads = [((ROWS * HI, DI), F32)] * SLOTS
    else:
        grads = [((GROUP * HI, DI), F32)]
    outputs = call(
        kernel,
        inputs,
        [((DI, HALF), F32)] * 2 + grads,
        [((ROWS * HI, HALF), BF16)] * 2,
        name="gradient_pass",
        flops=2 * GROUP * HI * DI * SHARD * 8,
        moved=4000000,
    )
    return outputs[0], outputs[1], outputs[2:] if final else outputs[2]


def pulled_from(value, axis, offset):
    size = lax.axis_size(axis)
    return lax.ppermute(value, axis, [((i + offset) % size, i) for i in range(size)])


def around(value, axis):
    return [value] + [pulled_from(value, axis, k) for k in range(1, lax.axis_size(axis))]


def gathered(low, high, axis):
    lows = {0: low, 1: pulled_from(low, axis, 1), 3: pulled_from(low, axis, -1)}
    highs = {0: high, 1: pulled_from(high, axis, 1), 3: pulled_from(high, axis, -1)}
    lows[2] = pulled_from(lows[1], axis, 1)
    highs[2] = pulled_from(highs[3], axis, -1)
    return lows, highs


def local(
    main_query, main_key, index_query, index_key, head_weight, query_positions, key_positions
):
    z, x, y, core = (lax.axis_index(name) for name in ("z", "x", "y", "c"))
    place = jnp.stack([z, x, core, y]).astype(jnp.int32)
    kpos = key_positions.reshape(128, 128)
    where = [place, query_positions, kpos]

    weights = jnp.pad(head_weight, ((0, 12), (0, DI - HI)))
    low, high = call(
        row_prep_kernel,
        [main_query.transpose(0, 2, 1), index_query.reshape(ROWS * HI, DI), weights],
        [((LOW_ROWS, H), BF16), ((HIGH_ROWS, H), BF16)],
        name="row_prep",
        moved=1300000,
    )
    row_low, row_high = gathered(low, high, "x")
    near_low, near_high, far_low, far_high = call(
        key_prep_kernel,
        [place, main_key.T, index_key],
        [((CUT, HALF), BF16)] * 4,
        name="key_prep",
        moved=3000000,
    )
    near_low, near_high = gathered(near_low, near_high, "z")
    far_low, far_high = {0: far_low}, {0: far_high}
    for step in (1, 3, 2):
        far_low[step] = pulled_from(near_low[step], "c", 1)
        far_high[step] = pulled_from(near_high[step], "c", 1)

    def key_inputs(steps):
        return [
            part[step] for step in steps for part in (near_low, near_high, far_low, far_high)
        ]

    def index_inputs(steps):
        return [part[step] for step in steps for part in (near_high, far_high)]

    queries = {slot: turn(slot, row_low[slot], row_high[slot]) for slot in (0, 1, 3)}
    (logits,) = call(
        index_first_kernel,
        where + [row_high[slot] for slot in NEAR] + index_inputs(NEAR),
        [((GROUP, SLOTS * SHARD), F32)],
        [((ROWS * HI, SHARD), F32)],
        name="index_first",
        flops=2 * 9 * ROWS * HI * DI * SHARD,
        moved=4000000,
    )
    first, stats = call(
        score_first_kernel,
        where + [queries[slot] for slot in NEAR] + key_inputs(NEAR),
        [((len(FIRST) * ROWS, H, SHARD), F32), ((SLOTS, H, 128), F32)],
        [((DEEP, SHARD), BF16)],
        name="score_first",
        flops=2 * 9 * ROWS * H * DK * SHARD,
        moved=20000000,
        exps=9 * ROWS * H * SHARD,
    )
    queries[2] = turn(2, row_low[2], row_high[2])
    logits, index_stats = call(
        index_last_kernel,
        where + [logits] + [row_high[slot] for slot in ALL] + index_inputs(ALL),
        [((GROUP, SLOTS * SHARD), F32), ((2 * GROUP, 128), F32)],
        [((ROWS * HI, SHARD), F32)],
        name="index_last",
        flops=2 * 7 * ROWS * HI * DI * SHARD,
        moved=4000000,
    )
    last, stats, message = call(
        score_last_kernel,
        where + [stats, index_stats] + [queries[slot] for slot in ALL] + key_inputs(ALL),
        [
            ((len(LAST) * ROWS, H, SHARD), F32),
            ((SLOTS, H, 128), F32),
            ((4 * GROUP, 128), F32),
        ],
        [((DEEP, SHARD), BF16)],
        name="score_last",
        flops=2 * 7 * ROWS * H * DK * SHARD,
        moved=16000000,
        exps=7 * ROWS * H * SHARD,
    )
    messages = around(message, "x")
    deltas, loss = call(
        target_kernel,
        messages + [stats, logits, first, last],
        [((GROUP, SLOTS * SHARD), F32), ((8, 128), F32)],
        [((GROUP, SLOTS * SHARD), F32)],
        name="target_pass",
        flops=2 * GROUP * H * SLOTS * SHARD,
        moved=34000000,
    )

    loss = sum(around(loss, "x"))
    loss = sum(around(loss, "z"))
    loss = sum(around(loss, "y"))
    loss = sum(around(loss, "c"))
    divergence = loss[0, 0] / ROW_TOTAL

    packs = [row_high[slot] for slot in ALL]
    query_grad = None
    key_parts = []
    for step in (2, 1, 3, 0):
        key_near, key_far, query_grad = gradient_pass(
            step, deltas, query_grad, packs, (near_high[step], far_high[step]), step == 0
        )
        mine = key_near + pulled_from(key_far, "c", 1)
        key_parts.append(pulled_from(mine, "z", -step) if step else mine)
    key_sum = sum(key_parts)
    blocks = [
        lax.dynamic_slice_in_dim(key_sum, lax.rem(y + k, 4) * 128, 128, 1) for k in range(4)
    ]
    key_total = blocks[0]
    for k in range(1, 4):
        key_total = key_total + pulled_from(blocks[k], "y", -k)

    row_total = query_grad[0]
    for k in range(1, SLOTS):
        row_total = row_total + pulled_from(query_grad[k], "x", -k)
    row_total = row_total.reshape(ROWS, HI, DI)
    grad_query = row_total * head_weight.astype(F32)[:, :, None]
    grad_weight = jnp.sum(row_total * index_query.astype(F32), axis=-1)
    return (divergence, grad_query, grad_weight, key_total.T)


def solution(mesh):
    fine = Mesh(mesh.devices.reshape(4, 4, 4, 2), ("z", "x", "y", "c"))
    rows = ("y", "c", "z", "x")
    keys = ("z", "x")
    return jax.shard_map(
        local,
        mesh=fine,
        in_specs=(
            P(rows, None, None),
            P(keys, None),
            P(rows, None, None),
            P(keys, None),
            P(rows, None),
            P(("y", "c")),
            P(),
        ),
        out_specs=(
            P(),
            P(rows, None, None),
            P(rows, None),
            P(("z", "x", "y", "c"), None),
        ),
        check_vma=False,
    )
```

```python
import jax
import jax.numpy as jnp
from jax import lax
from jax.experimental import pallas as pl
from jax.experimental.pallas import tpu as pltpu
from jax.sharding import Mesh, PartitionSpec as P

H = 128
DR = 64
DN = 128
HI = 64
DI = 128
DK = 576
ROWS = 4
SLOTS = 4
GROUP = ROWS * SLOTS
SHARD = 1024
HALF = SHARD // 2
DEEP = DK + GROUP
PACK = ROWS * HI + 16
SPLIT = 2 * DK + PACK
MESSAGE = 4 * DK + PACK
PACK_AT = 2 * DK
WIDTH = DK + DI
CUT = WIDTH // 2
ROW_TOTAL = 512
NEGATIVE = -1e30
LOG2E = 1.4426950408889634
SCALE2 = (DN + DR) ** (-0.5) * LOG2E
F32 = jnp.float32
BF16 = jnp.bfloat16
VMEM_LIMIT = 6 * 1024 * 1024
NEAR = (0, 1, 3)
ALL = (0, 1, 2, 3)
PHASES = (
    [(0, slot) for slot in NEAR],
    [(step, slot) for step in (1, 3) for slot in NEAR],
    [(step, 2) for step in NEAR],
    [(2, slot) for slot in ALL],
)


def call(kernel, inputs, outputs, scratch=(), name=None, flops=1, after=(), far=(), semaphores=0, room=VMEM_LIMIT):
    count = len(inputs) + len(far)

    def body(*refs):
        kernel(*refs[:count], *refs[count + len(after) :])

    return pl.pallas_call(
        body,
        in_specs=[
            pl.BlockSpec(memory_space=pltpu.SMEM if value.ndim == 1 else pltpu.VMEM)
            for value in inputs
        ]
        + [pl.BlockSpec(memory_space=pltpu.HBM)] * len(far)
        + [pl.BlockSpec(memory_space=pl.ANY)] * len(after),
        out_specs=[pl.BlockSpec(memory_space=pltpu.VMEM)] * len(outputs),
        out_shape=[jax.ShapeDtypeStruct(shape, dtype) for shape, dtype in outputs],
        scratch_shapes=[pltpu.VMEM(shape, dtype) for shape, dtype in scratch]
        + [pltpu.SemaphoreType.DMA((semaphores,))] * (semaphores > 0),
        compiler_params=pltpu.CompilerParams(vmem_limit_bytes=room),
        cost_estimate=pl.CostEstimate(flops=flops, bytes_accessed=1, transcendentals=0),
        name=name,
    )(*inputs, *far, *after)


def contract(a, b, dim_a, dim_b):
    return lax.dot_general(a, b, (((dim_a,), (dim_b,)), ((), ())), preferred_element_type=F32)


def largest(values):
    best = values[0]
    for value in values[1:]:
        best = jnp.maximum(best, value)
    return best


def row_position(place, qpos, slot, row):
    return qpos[place[0] * GROUP + lax.rem(place[1] + slot, SLOTS) * ROWS + row]


def key_positions_of(place, kpos, step):
    core = place[2]
    base = (lax.rem(place[0] + step, SLOTS) * SLOTS + place[1]) * 8
    pieces = [kpos[pl.ds(base + 2 * y + core, 1), :] for y in range(4)]
    pieces += [kpos[pl.ds(base + 2 * y + 1 - core, 1), :] for y in range(4)]
    return jnp.concatenate(pieces, axis=1)


def prep_kernel(place, weight, query, index_query, main_key, index_key, row, near, far, held, sems):
    core = place[2]
    copies = []

    def move(source, target):
        copies.append(pltpu.make_async_copy(source, target, sems.at[len(copies)]))
        copies[-1].start()

    move(index_key, held)
    for i in range(ROWS):
        move(query.at[i], row.at[pl.ds(i * DK + (PACK if i > 1 else 0), DK)])
    move(index_query, row.at[pl.ds(PACK_AT, ROWS * HI)])
    for y in range(4):
        for own, out in ((0, near), (1, far)):
            block = 2 * y + (core if own == 0 else 1 - core)
            start = pl.multiple_of(block * 128, 128)
            move(main_key.at[:, pl.ds(start, 128)], out.at[pl.ds(0, DK), pl.ds(y * 128, 128)])
    padded = jnp.concatenate([weight[...].astype(F32), jnp.zeros((ROWS, DI - HI), F32)], axis=1)
    padded = jnp.concatenate([padded, jnp.zeros((16 - ROWS, DI), F32)], axis=0)
    row[PACK_AT + ROWS * HI : SPLIT, :] = padded.astype(BF16)
    copies[0].wait()
    for y in range(4):
        for own, out in ((0, near), (1, far)):
            block = 2 * y + (core if own == 0 else 1 - core)
            start = pl.multiple_of(block * 128, 128)
            out[DK:, y * 128 : (y + 1) * 128] = held[pl.ds(start, 128), :].T
    for copy in copies[1:]:
        copy.wait()


def turn_kernel(slot, *refs):
    sources, turned = refs[:-1], refs[-1]
    lane = lax.broadcasted_iota(jnp.int32, (H, GROUP), 1)
    for row in range(ROWS):
        source, start = sources[0], row * DK
        if row > 1:
            source = sources[-1]
            start += PACK if len(sources) == 1 else PACK - SPLIT
        part = slice(row * H, (row + 1) * H)
        turned[part, :DK] = source[start : start + DK, :].T
        turned[part, DK:] = jnp.where(lane == slot * ROWS + row, 1.0, 0.0).astype(BF16)


def turn(slot, sources, after=()):
    return call(
        lambda *refs: turn_kernel(slot, *refs),
        sources,
        [((ROWS * H, DEEP), BF16)],
        name="turn",
        after=after,
    )[0]


def feature_rows(parts, start, stop):
    if len(parts) == 1:
        return [parts[0][start:stop, :]]
    pieces = []
    if start < CUT:
        pieces.append(parts[0][start : min(stop, CUT), :])
    if stop > CUT:
        pieces.append(parts[1][max(start, CUT) - CUT : stop - CUT, :])
    return pieces


def work_kernel(units, final, slots, steps, place, qpos, kpos, *refs):
    refs = list(refs)
    queries = {slot: refs.pop(0) for slot in slots}
    packs = {slot: refs.pop(0) for slot in slots}
    halves = {}
    for step in steps:
        count = 2 if step == 2 else 1
        halves[step] = [[refs.pop(0) for _ in range(count)] for _ in range(2)]
    logits_before = stats_before = None
    if units is not PHASES[0]:
        logits_before, stats_before = refs.pop(0), refs.pop(0)
    terms = [refs.pop(0) for _ in units]
    logits, stat_out = refs.pop(0), refs.pop(0)
    message = refs.pop(0) if final else None
    keys, scores = refs
    if logits_before is None:
        logits[...] = jnp.zeros(logits.shape, F32)
        stats = {step: jnp.zeros((H, 128), F32) for step in ALL}
    else:
        logits[...] = logits_before[...]
        stats = {step: stats_before[step] for step in ALL}
    lane = lax.broadcasted_iota(jnp.int32, (H, 128), 1)
    weights = {slot: packs[slot][PACK_AT + ROWS * HI : SPLIT, :].astype(F32).T for slot in slots}
    staged = None
    waiting = []

    def finish(unit, pair):
        step, slot = units[unit]
        for row in range(2 * pair, 2 * pair + 2):
            values = terms[unit][row]
            best = jnp.max(values, axis=1, keepdims=True)
            part = jnp.exp2((values - best) * SCALE2)
            total = jnp.sum(part, axis=1, keepdims=True)
            terms[unit][row] = part
            index = slot * ROWS + row
            stats[step] = jnp.where(
                lane == index, best, jnp.where(lane == GROUP + index, total, stats[step])
            )

    for unit, (step, slot) in enumerate(units):
        if staged != step:
            staged = step
            for side in range(2):
                part = slice(side * HALF, (side + 1) * HALF)
                at = 0
                for piece in feature_rows(halves[step][side], 0, DK):
                    keys[at : at + piece.shape[0], part] = piece
                    at += piece.shape[0]
            position = key_positions_of(place, kpos, step)
            hidden = [
                jnp.where(position <= row_position(place, qpos, i // ROWS, i % ROWS), 0.0, NEGATIVE)
                for i in range(GROUP)
            ]
            keys[DK:, :] = jnp.concatenate(hidden, axis=0).astype(BF16)
        index_queries = packs[slot][PACK_AT : PACK_AT + ROWS * HI, :]
        for side in range(2):
            (index_keys,) = feature_rows(halves[step][side], DK, WIDTH)
            scores[:, side * HALF : (side + 1) * HALF] = contract(index_queries, index_keys, 1, 0)
        for pair in range(2):
            part = slice(2 * pair * H, (2 * pair + 2) * H)
            product = contract(queries[slot][part, :], keys[...], 1, 0)
            terms[unit][2 * pair : 2 * pair + 2] = product.reshape(2, H, SHARD)
            if waiting:
                finish(*waiting.pop())
            waiting.append((unit, pair))
            for row in range(2 * pair, 2 * pair + 2):
                active = jnp.maximum(scores[row * HI : (row + 1) * HI, :], 0.0)
                line = jnp.sum(active * weights[slot][:HI, row : row + 1], axis=0, keepdims=True)
                visible = position <= row_position(place, qpos, slot, row)
                index = slot * ROWS + row
                logits[index : index + 1, step * SHARD : (step + 1) * SHARD] = jnp.where(
                    visible, line, NEGATIVE
                )
    finish(*waiting.pop())
    for step in ALL:
        stat_out[step] = stats[step]
    if not final:
        return
    best = largest([stats[step] for step in ALL])
    total = jnp.zeros((H, 128), F32)
    for step in ALL:
        factor = pltpu.roll(jnp.exp2((stats[step] - best) * SCALE2), GROUP, 1)
        total = total + stats[step] * jnp.where(
            (lane >= GROUP) & (lane < 2 * GROUP), factor, 0.0
        )
    both = jnp.where(lane < GROUP, best, total)
    message[: 2 * GROUP, :] = both.T[: 2 * GROUP, :]
    values = logits[...]
    best = jnp.max(values, axis=1, keepdims=True)
    total = jnp.sum(jnp.exp2((values - best) * LOG2E), axis=1, keepdims=True)
    message[2 * GROUP : 3 * GROUP, :] = jnp.broadcast_to(best, (GROUP, 128))
    message[3 * GROUP :, :] = jnp.broadcast_to(total, (GROUP, 128))


def work(phase, where, queries, packs, halves, carried, after=()):
    units = PHASES[phase]
    final = phase == len(PHASES) - 1
    slots = [slot for slot in ALL if any(unit[1] == slot for unit in units)]
    steps = [step for step in ALL if any(unit[0] == step for unit in units)]
    inputs = where + [queries[slot] for slot in slots] + [packs[slot] for slot in slots]
    for step in steps:
        inputs += halves[step][0] + halves[step][1]
    outputs = [((ROWS, H, SHARD), F32)] * len(units)
    outputs += [((GROUP, SLOTS * SHARD), F32), ((SLOTS, H, 128), F32)]
    if final:
        outputs.append(((4 * GROUP, 128), F32))
    results = call(
        lambda *refs: work_kernel(units, final, slots, steps, *refs),
        inputs + list(carried),
        outputs,
        [((DEEP, SHARD), BF16), ((ROWS * HI, SHARD), F32)],
        name="work",
        room=4 * 1024 * 1024,
        flops=2 * len(units) * ROWS * SHARD * (H * DK + HI * DI),
        after=after,
    )
    return results[: len(units)], results[len(units) :]


def target_kernel(*refs):
    messages, stats, logits = refs[:4], refs[4], refs[5]
    terms, (deltas, loss, target) = refs[6:-3], refs[-3:]

    def field(index):
        return [
            jnp.concatenate(
                [
                    message[pl.ds(index * GROUP + (i - k) % SLOTS * ROWS, ROWS), :]
                    for i in range(SLOTS)
                ],
                axis=0,
            )
            for k, message in enumerate(messages)
        ]

    maxima, totals = field(0), field(1)
    best = largest(maxima)
    total = jnp.zeros((GROUP, 128), F32)
    for k in range(SLOTS):
        total = total + totals[k] * jnp.exp2((maxima[k] - best) * SCALE2)
    both = jnp.concatenate([best, 1.0 / (total * H), jnp.zeros((96, 128), F32)], axis=0).T
    factors = [
        jnp.exp2((stats[step][:, :GROUP] - both[:, :GROUP]) * SCALE2) * both[:, GROUP : 2 * GROUP]
        for step in ALL
    ]
    units = [unit for phase in PHASES for unit in phase]
    for part, (step, slot) in zip(terms, units):
        for row in range(ROWS):
            at = slot * ROWS + row
            total = jnp.zeros((8, SHARD), F32)
            for start in range(0, H, 8):
                lines = slice(start, start + 8)
                total = total + part[row, lines, :] * factors[step][lines, at : at + 1]
            target[at : at + 1, step * SHARD : (step + 1) * SHARD] = jnp.sum(
                total, axis=0, keepdims=True
            )
    maxima, totals = field(2), field(3)
    best = largest(maxima)
    total = jnp.zeros((GROUP, 128), F32)
    for k in range(SLOTS):
        total = total + totals[k] * jnp.exp2((maxima[k] - best) * LOG2E)
    best, total = best[:, :1], total[:, :1]
    norm = best + jnp.log(total)
    share = 1.0 / total
    lost = jnp.zeros((GROUP, 1), F32)
    for step in range(SLOTS):
        columns = slice(step * SHARD, (step + 1) * SHARD)
        wanted = target[:, columns]
        value = logits[:, columns]
        prob = jnp.exp2((value - best) * LOG2E) * share
        deltas[:, columns] = prob - wanted
        pieces = wanted * (jnp.log(jnp.maximum(wanted, 1e-37)) - (value - norm))
        lost = lost + jnp.sum(jnp.where(wanted > 0, pieces, 0.0), axis=1, keepdims=True)
    loss[...] = jnp.broadcast_to(jnp.sum(lost, axis=0, keepdims=True), (8, 128))


def key_gradient_kernel(step, slots, chained, deltas, *refs):
    count = len(slots)
    packs, loss, refs = refs[:count], refs[count], refs[count + 1 :]
    before, refs = (refs[:2], refs[2:]) if chained else (None, refs)
    halves, (key_near, key_far, highs, lows) = refs[:-4], refs[-4:]
    sides = [halves[:1], halves[1:]] if len(halves) == 2 else [halves[:2], halves[2:]]
    total = [jnp.zeros((2 * DI, HALF), F32), jnp.zeros((2 * DI, HALF), F32)]
    for place, slot in enumerate(slots):
        queries = packs[place][PACK_AT : PACK_AT + ROWS * HI, :]
        weights = packs[place][PACK_AT + ROWS * HI : SPLIT, :].astype(F32).T
        product = jnp.concatenate(
            [
                queries[row * HI : (row + 1) * HI].astype(F32) * weights[:HI, row : row + 1]
                for row in range(ROWS)
            ],
            axis=0,
        )
        high = product.astype(BF16).astype(F32)
        both = jnp.concatenate([high.T, (product - high).T], axis=0).astype(BF16)
        part = slice(place * ROWS * HI, (place + 1) * ROWS * HI)
        for side in range(2):
            (keys,) = feature_rows(sides[side], DK, WIDTH)
            scores = contract(queries, keys, 1, 0)
            columns = slice(side * HALF, (side + 1) * HALF)
            for row in range(ROWS):
                at = slot * ROWS + row
                start = step * SHARD + side * HALF
                delta = deltas[at : at + 1, start : start + HALF]
                delta_high = delta.astype(BF16).astype(F32)
                delta_low = delta - delta_high
                active = scores[row * HI : (row + 1) * HI, :] > 0
                lines = slice((place * ROWS + row) * HI, (place * ROWS + row + 1) * HI)
                highs[lines, columns] = jnp.where(active, delta_high, 0.0).astype(BF16)
                lows[lines, columns] = jnp.where(active, delta_low, 0.0).astype(BF16)
            wide = contract(both, highs[part, columns], 1, 0)
            narrow = contract(both[:DI], lows[part, columns], 1, 0)
            total[side] = total[side] + jnp.concatenate([wide[:DI] + narrow, wide[DI:]], axis=0)
    for side, out in enumerate((key_near, key_far)):
        value = total[side][:DI] + total[side][DI:]
        out[:DI, :] = value + before[side][:DI, :] if chained else value
        out[DI:, :] = jnp.broadcast_to(loss[:, :1], (8, HALF))


def key_gradient(step, slots, deltas, loss, packs, halves, before=(), after=()):
    near, far, highs, lows = call(
        lambda *refs: key_gradient_kernel(step, slots, len(before) > 0, *refs),
        [deltas, *[packs[slot] for slot in slots], loss, *before, *halves[0], *halves[1]],
        [((DI + 8, HALF), F32)] * 2 + [((len(slots) * ROWS * HI, SHARD), BF16)] * 2,
        name="key_gradient",
        flops=len(slots) * 800000000,
        after=after,
    )
    masked = {(step, slot): (highs, lows, i * ROWS * HI) for i, slot in enumerate(slots)}
    return near, far, masked


def query_gradient_kernel(slots, starts, *refs):
    count = 2 * SLOTS * len(slots)
    masked, sides, outs = refs[:count], refs[count : -len(slots)], refs[-len(slots) :]
    sides = list(sides)
    keys = []
    for step in ALL:
        parts = 2 if step == 2 else 1
        for side in range(2):
            (rows,) = feature_rows([sides.pop(0) for _ in range(parts)], DK, WIDTH)
            keys.append(rows)
    for place, out in enumerate(outs):
        total = None
        for step in ALL:
            start = starts[place * SLOTS + step]
            for level in range(2):
                source = masked[2 * (place * SLOTS + step) + level]
                for side in range(2):
                    columns = slice(side * HALF, (side + 1) * HALF)
                    more = contract(
                        source[start : start + ROWS * HI, columns], keys[2 * step + side], 1, 1
                    )
                    total = more if total is None else total + more
        out[...] = total


def query_gradient(slots, masked, halves, after=()):
    pieces = [masked[step, slot] for slot in slots for step in ALL]
    starts = [piece[2] for piece in pieces]
    return call(
        lambda *refs: query_gradient_kernel(slots, starts, *refs),
        [level for piece in pieces for level in piece[:2]]
        + [part for step in ALL for half in halves[step] for part in half],
        [((ROWS * HI, DI), F32)] * len(slots),
        name="query_gradient",
        flops=len(slots) * 1300000000,
        after=after,
    )


def key_block_kernel(place, *refs):
    parts, outs = refs[:SLOTS], refs[SLOTS : 2 * SLOTS]
    total = refs[-1]
    total[...] = parts[0][...] + parts[1][...] + parts[2][...] + parts[3][...]
    for k in range(SLOTS):
        start = pl.multiple_of(lax.rem(place[3] + k, SLOTS) * 128, 128)
        outs[k][...] = total[:, pl.ds(start, 128)]


def pulled_from(value, axis, offset):
    size = lax.axis_size(axis)
    return lax.ppermute(value, axis, [((i + offset) % size, i) for i in range(size)])


def around(value, axis):
    return [value] + [pulled_from(value, axis, k) for k in range(1, lax.axis_size(axis))]


def local(
    main_query, main_key, index_query, index_key, head_weight, query_positions, key_positions
):
    z, x, y, core = (lax.axis_index(name) for name in ("z", "x", "y", "c"))
    place = jnp.stack([z, x, core, y]).astype(jnp.int32)
    kpos = key_positions.reshape(128, 128)
    where = [place, query_positions, kpos]

    row, near, far = call(
        prep_kernel,
        [place, head_weight],
        [((MESSAGE, H), BF16), ((WIDTH, HALF), BF16), ((WIDTH, HALF), BF16)],
        [((SHARD, DI), BF16)],
        name="prep",
        room=60 * 1024 * 1024,
        far=[
            main_query.transpose(0, 2, 1),
            index_query.reshape(ROWS * HI, DI),
            main_key.T,
            index_key,
        ],
        semaphores=14,
    )
    rows = {0: [row], 1: [pulled_from(row, "x", 1)], 3: [pulled_from(row, "x", -1)]}
    nears = {0: [near], 1: [pulled_from(near, "z", 1)], 3: [pulled_from(near, "z", -1)]}
    rows[2] = [pulled_from(rows[1][0][:SPLIT], "x", 1), pulled_from(rows[3][0][SPLIT:], "x", -1)]
    nears[2] = [pulled_from(nears[1][0][:CUT], "z", 1), pulled_from(nears[3][0][CUT:], "z", -1)]
    halves = {0: [[near], [far]]}
    for step in (1, 3, 2):
        halves[step] = [nears[step], [pulled_from(part, "c", 1) for part in nears[step]]]
    packs = {slot: rows[slot][0] for slot in ALL}

    queries = {slot: turn(slot, rows[slot]) for slot in NEAR}
    terms = []
    carried = ()
    for phase in range(len(PHASES)):
        if phase == 2:
            queries[2] = turn(2, rows[2], carried[1:])
        more, carried = work(phase, where, queries, packs, halves, carried)
        terms += more
    packs = [packs[slot] for slot in ALL]
    logits, stats, message = carried
    messages = around(message, "x")
    deltas, loss = call(
        target_kernel,
        messages + [stats, logits] + terms,
        [((GROUP, SLOTS * SHARD), F32), ((8, 128), F32)],
        [((GROUP, SLOTS * SHARD), F32)],
        name="target_pass",
        room=10 * 1024 * 1024,
    )

    masked = {}
    key_parts = {}
    sums = {}

    def gradient(step, slots, before=(), after=()):
        near, far, more = key_gradient(
            step, slots, deltas, loss, packs, halves[step], before, after
        )
        masked.update(more)
        return near, far

    def collect(step, near, far):
        sums[step] = near + pulled_from(far, "c", 1)
        key_parts[step] = pulled_from(sums[step], "z", -step) if step else sums[step]

    collect(2, *gradient(2, ALL))
    collect(1, *gradient(1, ALL))
    collect(3, *gradient(3, ALL, (), [sums[2]]))
    first = gradient(0, (0, 1), (), [sums[1]])
    collect(0, *gradient(0, (2, 3), first, [sums[3]]))
    grads = {}
    grads.update(zip((2, 1), query_gradient((2, 1), masked, halves, [key_parts[2], key_parts[1]])))
    blocks = call(
        key_block_kernel,
        [place] + [key_parts[step] for step in ALL],
        [((DI + 8, 128), F32)] * SLOTS,
        [((DI + 8, HALF), F32)],
        name="key_blocks",
    )
    grads.update(zip((3, 0), query_gradient((3, 0), masked, halves, blocks)))
    key_total = blocks[0]
    for k in range(1, 4):
        key_total = key_total + pulled_from(blocks[k], "y", -k)
    rows = {k: jnp.concatenate([grads[k], key_total[DI:]], axis=0) for k in ALL}
    row_total = rows[0]
    for k in range(1, SLOTS):
        row_total = row_total + pulled_from(rows[k], "x", -k)
    divergence = row_total[ROWS * HI, 0] / ROW_TOTAL
    row_total = row_total[: ROWS * HI]
    row_total = row_total.reshape(ROWS, HI, DI)
    grad_query = row_total * head_weight.astype(F32)[:, :, None]
    grad_weight = jnp.sum(row_total * index_query.astype(F32), axis=-1)
    return (divergence, grad_query, grad_weight, key_total[:DI].T)


def solution(mesh):
    fine = Mesh(mesh.devices.reshape(4, 4, 4, 2), ("z", "x", "y", "c"))
    rows = ("y", "c", "z", "x")
    keys = ("z", "x")
    return jax.shard_map(
        local,
        mesh=fine,
        in_specs=(
            P(rows, None, None),
            P(keys, None),
            P(rows, None, None),
            P(keys, None),
            P(rows, None),
            P(("y", "c")),
            P(),
        ),
        out_specs=(
            P(),
            P(rows, None, None),
            P(rows, None),
            P(("z", "x", "y", "c"), None),
        ),
        check_vma=False,
    )
```

```python
import jax
import jax.numpy as jnp
from jax import lax
from jax.experimental import pallas as pl
from jax.experimental.pallas import tpu as pltpu
from jax.sharding import Mesh, PartitionSpec as P

H = 128
DR = 64
DN = 128
HI = 64
DI = 128
DK = 576
ROWS = 4
SLOTS = 4
GROUP = ROWS * SLOTS
SHARD = 1024
HALF = SHARD // 2
DEEP = DK + GROUP
PACK = ROWS * HI + 16
SPLIT = 2 * DK + PACK
MESSAGE = 4 * DK + PACK
PACK_AT = 2 * DK
WIDTH = DK + DI
CUT = WIDTH // 2
ROW_TOTAL = 512
NEGATIVE = -1e30
LOG2E = 1.4426950408889634
SCALE2 = (DN + DR) ** (-0.5) * LOG2E
F32 = jnp.float32
BF16 = jnp.bfloat16
VMEM_LIMIT = 6 * 1024 * 1024
NEAR = (0, 1, 3)
ALL = (0, 1, 2, 3)
PHASES = (
    [(0, slot) for slot in NEAR],
    [(step, slot) for step in (1, 3) for slot in NEAR],
    [(step, 2) for step in NEAR],
    [(2, slot) for slot in ALL],
)


def call(kernel, inputs, outputs, scratch=(), name=None, flops=1, after=(), far=(), semaphores=0, room=VMEM_LIMIT):
    count = len(inputs) + len(far)

    def body(*refs):
        kernel(*refs[:count], *refs[count + len(after) :])

    return pl.pallas_call(
        body,
        in_specs=[
            pl.BlockSpec(memory_space=pltpu.SMEM if value.ndim == 1 else pltpu.VMEM)
            for value in inputs
        ]
        + [pl.BlockSpec(memory_space=pltpu.HBM)] * len(far)
        + [pl.BlockSpec(memory_space=pl.ANY)] * len(after),
        out_specs=[
            pl.BlockSpec(memory_space=pltpu.SMEM if len(shape) == 1 else pltpu.VMEM)
            for shape, _ in outputs
        ],
        out_shape=[jax.ShapeDtypeStruct(shape, dtype) for shape, dtype in outputs],
        scratch_shapes=[pltpu.VMEM(shape, dtype) for shape, dtype in scratch]
        + [pltpu.SemaphoreType.DMA((semaphores,))] * (semaphores > 0),
        compiler_params=pltpu.CompilerParams(vmem_limit_bytes=room),
        cost_estimate=pl.CostEstimate(flops=flops, bytes_accessed=1, transcendentals=0),
        name=name,
    )(*inputs, *far, *after)


def contract(a, b, dim_a, dim_b):
    return lax.dot_general(a, b, (((dim_a,), (dim_b,)), ((), ())), preferred_element_type=F32)


def largest(values):
    best = values[0]
    for value in values[1:]:
        best = jnp.maximum(best, value)
    return best


def row_position(place, qpos, slot, row):
    return qpos[place[0] * GROUP + lax.rem(place[1] + slot, SLOTS) * ROWS + row]


def key_positions_of(place, kpos, step):
    core = place[2]
    base = (lax.rem(place[0] + step, SLOTS) * SLOTS + place[1]) * 8
    pieces = [kpos[pl.ds(base + 2 * y + core, 1), :] for y in range(4)]
    pieces += [kpos[pl.ds(base + 2 * y + 1 - core, 1), :] for y in range(4)]
    return jnp.concatenate(pieces, axis=1)


def prep_kernel(place, weight, query, index_query, main_key, index_key, row, near, far, held, sems):
    core = place[2]
    copies = []

    def move(source, target):
        copies.append(pltpu.make_async_copy(source, target, sems.at[len(copies)]))
        copies[-1].start()

    move(index_key, held)
    for i in range(ROWS):
        move(query.at[i], row.at[pl.ds(i * DK + (PACK if i > 1 else 0), DK)])
    move(index_query, row.at[pl.ds(PACK_AT, ROWS * HI)])
    for y in range(4):
        for own, out in ((0, near), (1, far)):
            block = 2 * y + (core if own == 0 else 1 - core)
            start = pl.multiple_of(block * 128, 128)
            move(main_key.at[:, pl.ds(start, 128)], out.at[pl.ds(0, DK), pl.ds(y * 128, 128)])
    padded = jnp.concatenate([weight[...].astype(F32), jnp.zeros((ROWS, DI - HI), F32)], axis=1)
    padded = jnp.concatenate([padded, jnp.zeros((16 - ROWS, DI), F32)], axis=0)
    row[PACK_AT + ROWS * HI : SPLIT, :] = padded.astype(BF16)
    copies[0].wait()
    for y in range(4):
        for own, out in ((0, near), (1, far)):
            block = 2 * y + (core if own == 0 else 1 - core)
            start = pl.multiple_of(block * 128, 128)
            out[DK:, y * 128 : (y + 1) * 128] = held[pl.ds(start, 128), :].T
    for copy in copies[1:]:
        copy.wait()


def turn_kernel(slot, *refs):
    sources, (turned, pack) = refs[:-2], refs[-2:]
    pack[...] = sources[0][PACK_AT:SPLIT, :]
    lane = lax.broadcasted_iota(jnp.int32, (H, GROUP), 1)
    for row in range(ROWS):
        source, start = sources[0], row * DK
        if row > 1:
            source = sources[-1]
            start += PACK if len(sources) == 1 else PACK - SPLIT
        part = slice(row * H, (row + 1) * H)
        turned[part, :DK] = source[start : start + DK, :].T
        turned[part, DK:] = jnp.where(lane == slot * ROWS + row, 1.0, 0.0).astype(BF16)


def turn(slot, sources, after=()):
    return call(
        lambda *refs: turn_kernel(slot, *refs),
        sources,
        [((ROWS * H, DEEP), BF16), ((PACK, DI), BF16)],
        name="turn",
        after=after,
    )


def feature_rows(parts, start, stop):
    if len(parts) == 1:
        return [parts[0][start:stop, :]]
    pieces = []
    if start < CUT:
        pieces.append(parts[0][start : min(stop, CUT), :])
    if stop > CUT:
        pieces.append(parts[1][max(start, CUT) - CUT : stop - CUT, :])
    return pieces


FRESH = ((0,), (1, 3), (), (2,))


def work_kernel(units, final, slots, steps, fresh, place, qpos, kpos, *refs):
    refs = list(refs)
    queries = {slot: refs.pop(0) for slot in slots}
    packs = {slot: refs.pop(0) for slot in slots}
    halves = {}
    for step in steps:
        count = 2 if step == 2 else 1
        halves[step] = [[refs.pop(0) for _ in range(count)] for _ in range(2)]
    logits_before = stats_before = None
    if units is not PHASES[0]:
        logits_before, stats_before = refs.pop(0), refs.pop(0)
    terms = [refs.pop(0) for _ in units]
    index_out = {step: refs.pop(0) for step in fresh}
    logits, stat_out = refs.pop(0), refs.pop(0)
    message = refs.pop(0) if final else None
    keys, scores = refs
    if logits_before is None:
        logits[...] = jnp.zeros(logits.shape, F32)
        stats = {step: jnp.zeros((H, 128), F32) for step in ALL}
    else:
        logits[...] = logits_before[...]
        stats = {step: stats_before[step] for step in ALL}
    lane = lax.broadcasted_iota(jnp.int32, (H, 128), 1)
    weights = {slot: packs[slot][ROWS * HI :, :].astype(F32).T for slot in slots}
    staged = None
    waiting = []

    def finish(unit, pair):
        step, slot = units[unit]
        for row in range(2 * pair, 2 * pair + 2):
            values = terms[unit][row]
            best = jnp.max(values, axis=1, keepdims=True)
            part = jnp.exp2((values - best) * SCALE2)
            total = jnp.sum(part, axis=1, keepdims=True)
            terms[unit][row] = part
            index = slot * ROWS + row
            stats[step] = jnp.where(
                lane == index, best, jnp.where(lane == GROUP + index, total, stats[step])
            )

    for unit, (step, slot) in enumerate(units):
        if staged != step:
            staged = step
            for side in range(2):
                part = slice(side * HALF, (side + 1) * HALF)
                at = 0
                for piece in feature_rows(halves[step][side], 0, DK):
                    keys[at : at + piece.shape[0], part] = piece
                    at += piece.shape[0]
                if step in fresh:
                    (piece,) = feature_rows(halves[step][side], DK, WIDTH)
                    index_out[step][:, part] = piece
            position = key_positions_of(place, kpos, step)
            hidden = [
                jnp.where(position <= row_position(place, qpos, i // ROWS, i % ROWS), 0.0, NEGATIVE)
                for i in range(GROUP)
            ]
            keys[DK:, :] = jnp.concatenate(hidden, axis=0).astype(BF16)
        index_queries = packs[slot][: ROWS * HI, :]
        for side in range(2):
            (index_keys,) = feature_rows(halves[step][side], DK, WIDTH)
            scores[:, side * HALF : (side + 1) * HALF] = contract(index_queries, index_keys, 1, 0)
        for pair in range(2):
            part = slice(2 * pair * H, (2 * pair + 2) * H)
            product = contract(queries[slot][part, :], keys[...], 1, 0)
            terms[unit][2 * pair : 2 * pair + 2] = product.reshape(2, H, SHARD)
            if waiting:
                finish(*waiting.pop())
            waiting.append((unit, pair))
            for row in range(2 * pair, 2 * pair + 2):
                active = jnp.maximum(scores[row * HI : (row + 1) * HI, :], 0.0)
                line = jnp.sum(active * weights[slot][:HI, row : row + 1], axis=0, keepdims=True)
                visible = position <= row_position(place, qpos, slot, row)
                index = slot * ROWS + row
                logits[index : index + 1, step * SHARD : (step + 1) * SHARD] = jnp.where(
                    visible, line, NEGATIVE
                )
    finish(*waiting.pop())
    for step in ALL:
        stat_out[step] = stats[step]
    if not final:
        return
    best = largest([stats[step] for step in ALL])
    total = jnp.zeros((H, 128), F32)
    for step in ALL:
        factor = pltpu.roll(jnp.exp2((stats[step] - best) * SCALE2), GROUP, 1)
        total = total + stats[step] * jnp.where(
            (lane >= GROUP) & (lane < 2 * GROUP), factor, 0.0
        )
    both = jnp.where(lane < GROUP, best, total)
    message[: 2 * GROUP, :] = both.T[: 2 * GROUP, :]
    values = logits[...]
    best = jnp.max(values, axis=1, keepdims=True)
    total = jnp.sum(jnp.exp2((values - best) * LOG2E), axis=1, keepdims=True)
    message[2 * GROUP : 3 * GROUP, :] = jnp.broadcast_to(best, (GROUP, 128))
    message[3 * GROUP :, :] = jnp.broadcast_to(total, (GROUP, 128))


def work(phase, where, queries, packs, halves, carried, after=()):
    units = PHASES[phase]
    final = phase == len(PHASES) - 1
    slots = [slot for slot in ALL if any(unit[1] == slot for unit in units)]
    steps = [step for step in ALL if any(unit[0] == step for unit in units)]
    inputs = where + [queries[slot] for slot in slots] + [packs[slot] for slot in slots]
    for step in steps:
        inputs += halves[step][0] + halves[step][1]
    fresh = FRESH[phase]
    outputs = [((ROWS, H, SHARD), F32)] * len(units) + [((DI, SHARD), BF16)] * len(fresh)
    outputs += [((GROUP, SLOTS * SHARD), F32), ((SLOTS, H, 128), F32)]
    if final:
        outputs.append(((4 * GROUP, 128), F32))
    results = call(
        lambda *refs: work_kernel(units, final, slots, steps, fresh, *refs),
        inputs + list(carried),
        outputs,
        [((DEEP, SHARD), BF16), ((ROWS * HI, SHARD), F32)],
        name="work",
        room=4 * 1024 * 1024,
        flops=2 * len(units) * ROWS * SHARD * (H * DK + HI * DI),
        after=after,
    )
    end = len(units) + len(fresh)
    return results[: len(units)], dict(zip(fresh, results[len(units) : end])), results[end:]


def target_kernel(*refs):
    messages, stats, logits = refs[:4], refs[4], refs[5]
    terms, (deltas, loss, target) = refs[6:-3], refs[-3:]

    def field(index):
        return [
            jnp.concatenate(
                [
                    message[pl.ds(index * GROUP + (i - k) % SLOTS * ROWS, ROWS), :]
                    for i in range(SLOTS)
                ],
                axis=0,
            )
            for k, message in enumerate(messages)
        ]

    maxima, totals = field(0), field(1)
    best = largest(maxima)
    total = jnp.zeros((GROUP, 128), F32)
    for k in range(SLOTS):
        total = total + totals[k] * jnp.exp2((maxima[k] - best) * SCALE2)
    both = jnp.concatenate([best, 1.0 / (total * H), jnp.zeros((96, 128), F32)], axis=0).T
    factors = [
        jnp.exp2((stats[step][:, :GROUP] - both[:, :GROUP]) * SCALE2) * both[:, GROUP : 2 * GROUP]
        for step in ALL
    ]
    units = [unit for phase in PHASES for unit in phase]
    for part, (step, slot) in zip(terms, units):
        for row in range(ROWS):
            at = slot * ROWS + row
            total = jnp.zeros((8, SHARD), F32)
            for start in range(0, H, 8):
                lines = slice(start, start + 8)
                total = total + part[row, lines, :] * factors[step][lines, at : at + 1]
            target[at : at + 1, step * SHARD : (step + 1) * SHARD] = jnp.sum(
                total, axis=0, keepdims=True
            )
    maxima, totals = field(2), field(3)
    best = largest(maxima)
    total = jnp.zeros((GROUP, 128), F32)
    for k in range(SLOTS):
        total = total + totals[k] * jnp.exp2((maxima[k] - best) * LOG2E)
    best, total = best[:, :1], total[:, :1]
    norm = best + jnp.log(total)
    share = 1.0 / total
    lost = jnp.zeros((GROUP, 1), F32)
    for step in range(SLOTS):
        columns = slice(step * SHARD, (step + 1) * SHARD)
        wanted = target[:, columns]
        value = logits[:, columns]
        prob = jnp.exp2((value - best) * LOG2E) * share
        deltas[:, columns] = prob - wanted
        pieces = wanted * (jnp.log(jnp.maximum(wanted, 1e-37)) - (value - norm))
        lost = lost + jnp.sum(jnp.where(wanted > 0, pieces, 0.0), axis=1, keepdims=True)
    loss[...] = jnp.broadcast_to(jnp.sum(lost, axis=0, keepdims=True), (8, 128))


def mask_kernel(*refs):
    packs, (keys, out) = refs[:SLOTS], refs[SLOTS:]
    for slot in range(SLOTS):
        scores = contract(packs[slot][: ROWS * HI, :], keys[...], 1, 0)
        part = slice(slot * ROWS * HI, (slot + 1) * ROWS * HI)
        out[part, :] = jnp.where(scores > 0, 1.0, 0.0).astype(BF16)


def mask(packs, keys, after):
    return call(
        mask_kernel,
        packs + [keys],
        [((GROUP * HI, SHARD), BF16)],
        name="mask",
        flops=800000000,
        after=after,
    )[0]


def key_gradient_kernel(step, deltas, loss, active, *refs):
    packs, (key_near, key_far, highs, lows) = refs[:SLOTS], refs[SLOTS:]
    total = [jnp.zeros((2 * DI, HALF), F32), jnp.zeros((2 * DI, HALF), F32)]
    for slot in range(SLOTS):
        queries = packs[slot][: ROWS * HI, :]
        weights = packs[slot][ROWS * HI :, :].astype(F32).T
        product = jnp.concatenate(
            [
                queries[row * HI : (row + 1) * HI].astype(F32) * weights[:HI, row : row + 1]
                for row in range(ROWS)
            ],
            axis=0,
        )
        high = product.astype(BF16).astype(F32)
        both = jnp.concatenate([high.T, (product - high).T], axis=0).astype(BF16)
        part = slice(slot * ROWS * HI, (slot + 1) * ROWS * HI)
        for side in range(2):
            columns = slice(side * HALF, (side + 1) * HALF)
            for row in range(ROWS):
                at = slot * ROWS + row
                start = step * SHARD + side * HALF
                delta = deltas[at : at + 1, start : start + HALF]
                high = delta.astype(BF16)
                low = (delta - high.astype(F32)).astype(BF16)
                lines = slice(at * HI, (at + 1) * HI)
                highs[lines, columns] = active[lines, columns] * high
                lows[lines, columns] = active[lines, columns] * low
            wide = contract(both, highs[part, columns], 1, 0)
            narrow = contract(both[:DI], lows[part, columns], 1, 0)
            total[side] = total[side] + jnp.concatenate([wide[:DI] + narrow, wide[DI:]], axis=0)
    for side, out in enumerate((key_near, key_far)):
        out[:DI, :] = total[side][:DI] + total[side][DI:]
        out[DI:, :] = jnp.broadcast_to(loss[:, :1], (8, HALF))


def key_gradient(step, deltas, loss, active, packs, after=()):
    near, far, *masked = call(
        lambda *refs: key_gradient_kernel(step, *refs),
        [deltas, loss, active, *packs],
        [((DI + 8, HALF), F32)] * 2 + [((GROUP * HI, SHARD), BF16)] * 2,
        name="key_gradient",
        flops=1600000000,
        after=after,
    )
    return near, far, masked


def query_gradient_kernel(slots, *refs):
    masked, keys, outs = refs[: 2 * SLOTS], refs[2 * SLOTS : 3 * SLOTS], refs[3 * SLOTS :]
    for slot, out in zip(slots, outs):
        part = slice(slot * ROWS * HI, (slot + 1) * ROWS * HI)
        total = jnp.zeros((ROWS * HI, DI), F32)
        for step in ALL:
            for level in range(2):
                total = total + contract(masked[2 * step + level][part, :], keys[step][...], 1, 1)
        out[...] = total


def query_gradient(slots, masked, keys, after=()):
    return call(
        lambda *refs: query_gradient_kernel(slots, *refs),
        [level for step in ALL for level in masked[step]] + [keys[step] for step in ALL],
        [((ROWS * HI, DI), F32)] * len(slots),
        name="query_gradient",
        flops=len(slots) * 1300000000,
        after=after,
    )


def key_block_kernel(place, *refs):
    parts, outs = refs[:SLOTS], refs[SLOTS : 2 * SLOTS]
    total = refs[-1]
    total[...] = parts[0][...] + parts[1][...] + parts[2][...] + parts[3][...]
    for k in range(SLOTS):
        start = pl.multiple_of(lax.rem(place[3] + k, SLOTS) * 128, 128)
        outs[k][...] = total[:, pl.ds(start, 128)]


def seal_kernel(*refs):
    parts, grads, (key_out, *messages) = refs[:SLOTS], refs[SLOTS : 2 * SLOTS], refs[2 * SLOTS :]
    total = parts[0][...] + parts[1][...] + parts[2][...] + parts[3][...]
    key_out[...] = total[:DI].T
    for grad, message in zip(grads, messages):
        message[: ROWS * HI, :] = grad[...]
        message[ROWS * HI :, :] = total[DI:]


def finish_kernel(pack, *refs):
    parts, (query_out, weight_out, divergence) = refs[:SLOTS], refs[SLOTS:]
    total = parts[0][...] + parts[1][...] + parts[2][...] + parts[3][...]
    divergence[0] = jnp.max(total[ROWS * HI :, :]) * (1.0 / ROW_TOTAL)
    grad = total[: ROWS * HI]
    queries = pack[: ROWS * HI, :].astype(F32)
    weights = pack[ROWS * HI :, :].astype(F32).T
    line = jnp.sum((queries * grad).T, axis=0, keepdims=True)
    for row in range(ROWS):
        part = slice(row * HI, (row + 1) * HI)
        query_out[part, :] = grad[part] * weights[:HI, row : row + 1]
        weight_out[row : row + 1, :] = line[:, part]


def pulled_from(value, axis, offset):
    size = lax.axis_size(axis)
    return lax.ppermute(value, axis, [((i + offset) % size, i) for i in range(size)])


def around(value, axis):
    return [value] + [pulled_from(value, axis, k) for k in range(1, lax.axis_size(axis))]


def local(
    main_query, main_key, index_query, index_key, head_weight, query_positions, key_positions
):
    z, x, y, core = (lax.axis_index(name) for name in ("z", "x", "y", "c"))
    place = jnp.stack([z, x, core, y]).astype(jnp.int32)
    kpos = key_positions.reshape(128, 128)
    where = [place, query_positions, kpos]

    row, near, far = call(
        prep_kernel,
        [place, head_weight],
        [((MESSAGE, H), BF16), ((WIDTH, HALF), BF16), ((WIDTH, HALF), BF16)],
        [((SHARD, DI), BF16)],
        name="prep",
        room=60 * 1024 * 1024,
        far=[
            main_query.transpose(0, 2, 1),
            index_query.reshape(ROWS * HI, DI),
            main_key.T,
            index_key,
        ],
        semaphores=14,
    )
    rows = {0: [row], 1: [pulled_from(row, "x", 1)], 3: [pulled_from(row, "x", -1)]}
    nears = {0: [near], 1: [pulled_from(near, "z", 1)], 3: [pulled_from(near, "z", -1)]}
    rows[2] = [pulled_from(rows[1][0][:SPLIT], "x", 1), pulled_from(rows[3][0][SPLIT:], "x", -1)]
    nears[2] = [pulled_from(nears[1][0][:CUT], "z", 1), pulled_from(nears[3][0][CUT:], "z", -1)]
    halves = {0: [[near], [far]]}
    for step in (1, 3, 2):
        halves[step] = [nears[step], [pulled_from(part, "c", 1) for part in nears[step]]]

    queries, packs, index_keys = {}, {}, {}
    for slot in NEAR:
        queries[slot], packs[slot] = turn(slot, rows[slot])
    terms = []
    carried = ()
    for phase in range(len(PHASES)):
        if phase == 2:
            queries[2], packs[2] = turn(2, rows[2], carried[1:])
        more, found, carried = work(phase, where, queries, packs, halves, carried)
        index_keys.update(found)
        terms += more
    packs = [packs[slot] for slot in ALL]
    logits, stats, message = carried
    messages = around(message, "x")
    ready = {step: mask(packs, index_keys[step], [message]) for step in (2, 1, 3, 0)}
    deltas, loss = call(
        target_kernel,
        messages + [stats, logits] + terms,
        [((GROUP, SLOTS * SHARD), F32), ((8, 128), F32)],
        [((GROUP, SLOTS * SHARD), F32)],
        name="target_pass",
        after=list(ready.values()),
        room=10 * 1024 * 1024,
    )

    masked = {}
    key_parts = {}
    sums = {}

    def gradient(step, after=()):
        near, far, masked[step] = key_gradient(step, deltas, loss, ready[step], packs, after)
        sums[step] = near + pulled_from(far, "c", 1)
        key_parts[step] = pulled_from(sums[step], "z", -step) if step else sums[step]

    gradient(2)
    gradient(1)
    gradient(3, [sums[2]])
    gradient(0, [sums[1]])
    grads = {}
    grads.update(zip((2, 1), query_gradient((2, 1), masked, index_keys, [sums[0], sums[3]])))
    blocks = call(
        key_block_kernel,
        [place] + [key_parts[step] for step in ALL],
        [((DI + 8, 128), F32)] * SLOTS,
        [((DI + 8, HALF), F32)],
        name="key_blocks",
        after=[grads[1]],
    )
    grads.update(zip((3, 0), query_gradient((3, 0), masked, index_keys, blocks)))
    parts = [blocks[0]] + [pulled_from(blocks[k], "y", -k) for k in range(1, SLOTS)]
    key_total, *rows = call(
        seal_kernel,
        parts + [grads[slot] for slot in ALL],
        [((DI, DI), F32)] + [((ROWS * HI + 8, DI), F32)] * SLOTS,
        name="seal",
    )
    rows = [rows[0]] + [pulled_from(rows[k], "x", -k) for k in range(1, SLOTS)]
    grad_query, grad_weight, divergence = call(
        finish_kernel,
        [packs[0]] + rows,
        [((ROWS * HI, DI), F32), ((ROWS, HI), F32), ((1,), F32)],
        name="finish",
    )
    return (
        divergence.reshape(()),
        grad_query.reshape(ROWS, HI, DI),
        grad_weight,
        key_total,
    )


def solution(mesh):
    fine = Mesh(mesh.devices.reshape(4, 4, 4, 2), ("z", "x", "y", "c"))
    rows = ("y", "c", "z", "x")
    keys = ("z", "x")
    return jax.shard_map(
        local,
        mesh=fine,
        in_specs=(
            P(rows, None, None),
            P(keys, None),
            P(rows, None, None),
            P(keys, None),
            P(rows, None),
            P(("y", "c")),
            P(),
        ),
        out_specs=(
            P(),
            P(rows, None, None),
            P(rows, None),
            P(("z", "x", "y", "c"), None),
        ),
        check_vma=False,
    )
```

```python
import jax
import jax.numpy as jnp
from jax import lax
from jax.experimental import pallas as pl
from jax.experimental.pallas import tpu as pltpu
from jax.sharding import Mesh, PartitionSpec as P

H = 128
DR = 64
DN = 128
HI = 64
DI = 128
DK = 576
ROWS = 4
SLOTS = 4
GROUP = ROWS * SLOTS
SHARD = 1024
HALF = SHARD // 2
DEEP = DK + GROUP
PACK = ROWS * HI + 16
SPLIT = 2 * DK + PACK
MESSAGE = 4 * DK + PACK
PACK_AT = 2 * DK
WIDTH = DK + DI
CUT = WIDTH // 2
ROW_TOTAL = 512
NEGATIVE = -1e30
LOG2E = 1.4426950408889634
SCALE2 = (DN + DR) ** (-0.5) * LOG2E
F32 = jnp.float32
BF16 = jnp.bfloat16
VMEM_LIMIT = 6 * 1024 * 1024
NEAR = (0, 1, 3)
ALL = (0, 1, 2, 3)
PHASES = (
    [(0, slot) for slot in NEAR],
    [(step, slot) for step in (1, 3) for slot in NEAR],
    [(step, 2) for step in NEAR],
    [(2, slot) for slot in ALL],
)


def call(kernel, inputs, outputs, scratch=(), name=None, flops=1, after=(), far=(), semaphores=0, room=VMEM_LIMIT):
    count = len(inputs) + len(far)

    def body(*refs):
        kernel(*refs[:count], *refs[count + len(after) :])

    return pl.pallas_call(
        body,
        in_specs=[
            pl.BlockSpec(memory_space=pltpu.SMEM if value.ndim == 1 else pltpu.VMEM)
            for value in inputs
        ]
        + [pl.BlockSpec(memory_space=pltpu.HBM)] * len(far)
        + [pl.BlockSpec(memory_space=pl.ANY)] * len(after),
        out_specs=[
            pl.BlockSpec(memory_space=pltpu.SMEM if len(shape) == 1 else pltpu.VMEM)
            for shape, _ in outputs
        ],
        out_shape=[jax.ShapeDtypeStruct(shape, dtype) for shape, dtype in outputs],
        scratch_shapes=[pltpu.VMEM(shape, dtype) for shape, dtype in scratch]
        + [pltpu.SemaphoreType.DMA((semaphores,))] * (semaphores > 0),
        compiler_params=pltpu.CompilerParams(vmem_limit_bytes=room),
        cost_estimate=pl.CostEstimate(flops=flops, bytes_accessed=1, transcendentals=0),
        name=name,
    )(*inputs, *far, *after)


def contract(a, b, dim_a, dim_b):
    return lax.dot_general(a, b, (((dim_a,), (dim_b,)), ((), ())), preferred_element_type=F32)


def largest(values):
    best = values[0]
    for value in values[1:]:
        best = jnp.maximum(best, value)
    return best


def row_position(place, qpos, slot, row):
    return qpos[place[0] * GROUP + lax.rem(place[1] + slot, SLOTS) * ROWS + row]


def key_positions_of(place, kpos, step):
    core = place[2]
    base = (lax.rem(place[0] + step, SLOTS) * SLOTS + place[1]) * 8
    pieces = [kpos[pl.ds(base + 2 * y + core, 1), :] for y in range(4)]
    pieces += [kpos[pl.ds(base + 2 * y + 1 - core, 1), :] for y in range(4)]
    return jnp.concatenate(pieces, axis=1)


def prep_kernel(place, weight, query, index_query, main_key, index_key, row, near, far, held, sems):
    core = place[2]
    copies = []

    def move(source, target):
        copies.append(pltpu.make_async_copy(source, target, sems.at[len(copies)]))
        copies[-1].start()

    move(index_key, held)
    for i in range(ROWS):
        move(query.at[i], row.at[pl.ds(i * DK + (PACK if i > 1 else 0), DK)])
    move(index_query, row.at[pl.ds(PACK_AT, ROWS * HI)])
    for y in range(4):
        for own, out in ((0, near), (1, far)):
            block = 2 * y + (core if own == 0 else 1 - core)
            start = pl.multiple_of(block * 128, 128)
            move(main_key.at[:, pl.ds(start, 128)], out.at[pl.ds(0, DK), pl.ds(y * 128, 128)])
    padded = jnp.concatenate([weight[...].astype(F32), jnp.zeros((ROWS, DI - HI), F32)], axis=1)
    padded = jnp.concatenate([padded, jnp.zeros((16 - ROWS, DI), F32)], axis=0)
    row[PACK_AT + ROWS * HI : SPLIT, :] = padded.astype(BF16)
    copies[0].wait()
    for y in range(4):
        for own, out in ((0, near), (1, far)):
            block = 2 * y + (core if own == 0 else 1 - core)
            start = pl.multiple_of(block * 128, 128)
            out[DK:, y * 128 : (y + 1) * 128] = held[pl.ds(start, 128), :].T
    for copy in copies[1:]:
        copy.wait()


def turn_kernel(slot, *refs):
    sources, (turned, pack) = refs[:-2], refs[-2:]
    pack[...] = sources[0][PACK_AT:SPLIT, :]
    lane = lax.broadcasted_iota(jnp.int32, (H, GROUP), 1)
    for row in range(ROWS):
        source, start = sources[0], row * DK
        if row > 1:
            source = sources[-1]
            start += PACK if len(sources) == 1 else PACK - SPLIT
        part = slice(row * H, (row + 1) * H)
        turned[part, :DK] = source[start : start + DK, :].T
        turned[part, DK:] = jnp.where(lane == slot * ROWS + row, 1.0, 0.0).astype(BF16)


def turn(slot, sources, after=()):
    return call(
        lambda *refs: turn_kernel(slot, *refs),
        sources,
        [((ROWS * H, DEEP), BF16), ((PACK, DI), BF16)],
        name="turn",
        after=after,
    )


def feature_rows(parts, start, stop):
    if len(parts) == 1:
        return [parts[0][start:stop, :]]
    pieces = []
    if start < CUT:
        pieces.append(parts[0][start : min(stop, CUT), :])
    if stop > CUT:
        pieces.append(parts[1][max(start, CUT) - CUT : stop - CUT, :])
    return pieces


FRESH = ((0,), (1, 3), (), (2,))


def work_kernel(units, final, slots, steps, fresh, place, qpos, kpos, *refs):
    refs = list(refs)
    queries = {slot: refs.pop(0) for slot in slots}
    packs = {slot: refs.pop(0) for slot in slots}
    halves = {}
    for step in steps:
        count = 2 if step == 2 else 1
        halves[step] = [[refs.pop(0) for _ in range(count)] for _ in range(2)]
    logits_before = stats_before = None
    if units is not PHASES[0]:
        logits_before, stats_before = refs.pop(0), refs.pop(0)
    terms = [refs.pop(0) for _ in units]
    index_out = {step: refs.pop(0) for step in fresh}
    logits, stat_out = refs.pop(0), refs.pop(0)
    message = refs.pop(0) if final else None
    keys, scores = refs
    if logits_before is None:
        logits[...] = jnp.zeros(logits.shape, F32)
        stats = {step: jnp.zeros((H, 128), F32) for step in ALL}
    else:
        logits[...] = logits_before[...]
        stats = {step: stats_before[step] for step in ALL}
    lane = lax.broadcasted_iota(jnp.int32, (H, 128), 1)
    weights = {slot: packs[slot][ROWS * HI :, :].astype(F32).T for slot in slots}
    staged = None
    waiting = []

    def finish(unit, pair):
        step, slot = units[unit]
        for row in range(2 * pair, 2 * pair + 2):
            values = terms[unit][row]
            best = jnp.max(values, axis=1, keepdims=True)
            part = jnp.exp2((values - best) * SCALE2)
            total = jnp.sum(part, axis=1, keepdims=True)
            terms[unit][row] = part
            index = slot * ROWS + row
            stats[step] = jnp.where(
                lane == index, best, jnp.where(lane == GROUP + index, total, stats[step])
            )

    for unit, (step, slot) in enumerate(units):
        if staged != step:
            staged = step
            for side in range(2):
                part = slice(side * HALF, (side + 1) * HALF)
                at = 0
                for piece in feature_rows(halves[step][side], 0, DK):
                    keys[at : at + piece.shape[0], part] = piece
                    at += piece.shape[0]
                if step in fresh:
                    (piece,) = feature_rows(halves[step][side], DK, WIDTH)
                    index_out[step][:, part] = piece
            position = key_positions_of(place, kpos, step)
            hidden = [
                jnp.where(position <= row_position(place, qpos, i // ROWS, i % ROWS), 0.0, NEGATIVE)
                for i in range(GROUP)
            ]
            keys[DK:, :] = jnp.concatenate(hidden, axis=0).astype(BF16)
        index_queries = packs[slot][: ROWS * HI, :]
        for side in range(2):
            (index_keys,) = feature_rows(halves[step][side], DK, WIDTH)
            scores[:, side * HALF : (side + 1) * HALF] = contract(index_queries, index_keys, 1, 0)
        for pair in range(2):
            part = slice(2 * pair * H, (2 * pair + 2) * H)
            product = contract(queries[slot][part, :], keys[...], 1, 0)
            terms[unit][2 * pair : 2 * pair + 2] = product.reshape(2, H, SHARD)
            if waiting:
                finish(*waiting.pop())
            waiting.append((unit, pair))
            for row in range(2 * pair, 2 * pair + 2):
                active = jnp.maximum(scores[row * HI : (row + 1) * HI, :], 0.0)
                line = jnp.sum(active * weights[slot][:HI, row : row + 1], axis=0, keepdims=True)
                visible = position <= row_position(place, qpos, slot, row)
                index = slot * ROWS + row
                logits[index : index + 1, step * SHARD : (step + 1) * SHARD] = jnp.where(
                    visible, line, NEGATIVE
                )
    finish(*waiting.pop())
    for step in ALL:
        stat_out[step] = stats[step]
    if not final:
        return
    best = largest([stats[step] for step in ALL])
    total = jnp.zeros((H, 128), F32)
    for step in ALL:
        factor = pltpu.roll(jnp.exp2((stats[step] - best) * SCALE2), GROUP, 1)
        total = total + stats[step] * jnp.where(
            (lane >= GROUP) & (lane < 2 * GROUP), factor, 0.0
        )
    both = jnp.where(lane < GROUP, best, total)
    message[: 2 * GROUP, :] = both.T[: 2 * GROUP, :]
    values = logits[...]
    best = jnp.max(values, axis=1, keepdims=True)
    total = jnp.sum(jnp.exp2((values - best) * LOG2E), axis=1, keepdims=True)
    message[2 * GROUP : 3 * GROUP, :] = jnp.broadcast_to(best, (GROUP, 128))
    message[3 * GROUP :, :] = jnp.broadcast_to(total, (GROUP, 128))


def work(phase, where, queries, packs, halves, carried, after=()):
    units = PHASES[phase]
    final = phase == len(PHASES) - 1
    slots = [slot for slot in ALL if any(unit[1] == slot for unit in units)]
    steps = [step for step in ALL if any(unit[0] == step for unit in units)]
    inputs = where + [queries[slot] for slot in slots] + [packs[slot] for slot in slots]
    for step in steps:
        inputs += halves[step][0] + halves[step][1]
    fresh = FRESH[phase]
    outputs = [((ROWS, H, SHARD), F32)] * len(units) + [((DI, SHARD), BF16)] * len(fresh)
    outputs += [((GROUP, SLOTS * SHARD), F32), ((SLOTS, H, 128), F32)]
    if final:
        outputs.append(((4 * GROUP, 128), F32))
    results = call(
        lambda *refs: work_kernel(units, final, slots, steps, fresh, *refs),
        inputs + list(carried),
        outputs,
        [((DEEP, SHARD), BF16), ((ROWS * HI, SHARD), F32)],
        name="work",
        room=4 * 1024 * 1024,
        flops=2 * len(units) * ROWS * SHARD * (H * DK + HI * DI),
        after=after,
    )
    end = len(units) + len(fresh)
    return results[: len(units)], dict(zip(fresh, results[len(units) : end])), results[end:]


def target_kernel(*refs):
    messages, stats, logits = refs[:4], refs[4], refs[5]
    terms, (deltas, loss, target) = refs[6:-3], refs[-3:]

    def field(index):
        return [
            jnp.concatenate(
                [
                    message[pl.ds(index * GROUP + (i - k) % SLOTS * ROWS, ROWS), :]
                    for i in range(SLOTS)
                ],
                axis=0,
            )
            for k, message in enumerate(messages)
        ]

    maxima, totals = field(0), field(1)
    best = largest(maxima)
    total = jnp.zeros((GROUP, 128), F32)
    for k in range(SLOTS):
        total = total + totals[k] * jnp.exp2((maxima[k] - best) * SCALE2)
    both = jnp.concatenate([best, 1.0 / (total * H), jnp.zeros((96, 128), F32)], axis=0).T
    factors = [
        jnp.exp2((stats[step][:, :GROUP] - both[:, :GROUP]) * SCALE2) * both[:, GROUP : 2 * GROUP]
        for step in ALL
    ]
    units = [unit for phase in PHASES for unit in phase]
    for part, (step, slot) in zip(terms, units):
        for row in range(ROWS):
            at = slot * ROWS + row
            total = jnp.zeros((8, SHARD), F32)
            for start in range(0, H, 8):
                lines = slice(start, start + 8)
                total = total + part[row, lines, :] * factors[step][lines, at : at + 1]
            target[at : at + 1, step * SHARD : (step + 1) * SHARD] = jnp.sum(
                total, axis=0, keepdims=True
            )
    maxima, totals = field(2), field(3)
    best = largest(maxima)
    total = jnp.zeros((GROUP, 128), F32)
    for k in range(SLOTS):
        total = total + totals[k] * jnp.exp2((maxima[k] - best) * LOG2E)
    best, total = best[:, :1], total[:, :1]
    norm = best + jnp.log(total)
    share = 1.0 / total
    lost = jnp.zeros((GROUP, 1), F32)
    for step in range(SLOTS):
        columns = slice(step * SHARD, (step + 1) * SHARD)
        wanted = target[:, columns]
        value = logits[:, columns]
        prob = jnp.exp2((value - best) * LOG2E) * share
        deltas[:, columns] = prob - wanted
        pieces = wanted * (jnp.log(jnp.maximum(wanted, 1e-37)) - (value - norm))
        lost = lost + jnp.sum(jnp.where(wanted > 0, pieces, 0.0), axis=1, keepdims=True)
    loss[...] = jnp.broadcast_to(jnp.sum(lost, axis=0, keepdims=True), (8, 128))


def mask_kernel(*refs):
    packs, (keys, out) = refs[:SLOTS], refs[SLOTS:]
    for slot in range(SLOTS):
        scores = contract(packs[slot][: ROWS * HI, :], keys[...], 1, 0)
        part = slice(slot * ROWS * HI, (slot + 1) * ROWS * HI)
        out[part, :] = jnp.where(scores > 0, 1.0, 0.0).astype(BF16)


def mask(packs, keys, after):
    return call(
        mask_kernel,
        packs + [keys],
        [((GROUP * HI, SHARD), BF16)],
        name="mask",
        flops=800000000,
        after=after,
    )[0]


def key_gradient_kernel(step, deltas, loss, active, *refs):
    packs, (key_near, key_far, highs, lows) = refs[:SLOTS], refs[SLOTS:]
    total = [jnp.zeros((2 * DI, HALF), F32), jnp.zeros((2 * DI, HALF), F32)]
    for slot in range(SLOTS):
        queries = packs[slot][: ROWS * HI, :]
        weights = packs[slot][ROWS * HI :, :].astype(F32).T
        product = jnp.concatenate(
            [
                queries[row * HI : (row + 1) * HI].astype(F32) * weights[:HI, row : row + 1]
                for row in range(ROWS)
            ],
            axis=0,
        )
        high = product.astype(BF16).astype(F32)
        both = jnp.concatenate([high.T, (product - high).T], axis=0).astype(BF16)
        part = slice(slot * ROWS * HI, (slot + 1) * ROWS * HI)
        for side in range(2):
            columns = slice(side * HALF, (side + 1) * HALF)
            for row in range(ROWS):
                at = slot * ROWS + row
                start = step * SHARD + side * HALF
                delta = deltas[at : at + 1, start : start + HALF]
                high = delta.astype(BF16)
                low = (delta - high.astype(F32)).astype(BF16)
                lines = slice(at * HI, (at + 1) * HI)
                highs[lines, columns] = active[lines, columns] * high
                lows[lines, columns] = active[lines, columns] * low
            wide = contract(both, highs[part, columns], 1, 0)
            narrow = contract(both[:DI], lows[part, columns], 1, 0)
            total[side] = total[side] + jnp.concatenate([wide[:DI] + narrow, wide[DI:]], axis=0)
    for side, out in enumerate((key_near, key_far)):
        out[:DI, :] = total[side][:DI] + total[side][DI:]
        out[DI:, :] = jnp.broadcast_to(loss[:, :1], (8, HALF))


def key_gradient(step, deltas, loss, active, packs, after=()):
    near, far, *masked = call(
        lambda *refs: key_gradient_kernel(step, *refs),
        [deltas, loss, active, *packs],
        [((DI + 8, HALF), F32)] * 2 + [((GROUP * HI, SHARD), BF16)] * 2,
        name="key_gradient",
        flops=1600000000,
        after=after,
    )
    return near, far, masked


def query_gradient_kernel(slots, *refs):
    masked, keys, outs = refs[: 2 * SLOTS], refs[2 * SLOTS : 3 * SLOTS], refs[3 * SLOTS :]
    for slot, out in zip(slots, outs):
        part = slice(slot * ROWS * HI, (slot + 1) * ROWS * HI)
        total = jnp.zeros((ROWS * HI, DI), F32)
        for step in ALL:
            for level in range(2):
                total = total + contract(masked[2 * step + level][part, :], keys[step][...], 1, 1)
        out[...] = total


def query_gradient(slots, masked, keys, after=()):
    return call(
        lambda *refs: query_gradient_kernel(slots, *refs),
        [level for step in ALL for level in masked[step]] + [keys[step] for step in ALL],
        [((ROWS * HI, DI), F32)] * len(slots),
        name="query_gradient",
        flops=len(slots) * 1300000000,
        after=after,
    )


def key_block_kernel(place, *refs):
    parts, outs = refs[:SLOTS], refs[SLOTS : 2 * SLOTS]
    total = refs[-1]
    total[...] = parts[0][...] + parts[1][...] + parts[2][...] + parts[3][...]
    for k in range(SLOTS):
        start = pl.multiple_of(lax.rem(place[3] + k, SLOTS) * 128, 128)
        outs[k][...] = total[:, pl.ds(start, 128)]


def seal_kernel(*refs):
    parts, (key_out, tile) = refs[:SLOTS], refs[SLOTS:]
    total = parts[0][...] + parts[1][...] + parts[2][...] + parts[3][...]
    key_out[...] = total[:DI].T
    tile[...] = total[DI:]


def finish_kernel(pack, *refs):
    parts, (query_out, weight_out) = refs[:SLOTS], refs[SLOTS:]
    grad = parts[0][...] + parts[1][...] + parts[2][...] + parts[3][...]
    queries = pack[: ROWS * HI, :].astype(F32)
    weights = pack[ROWS * HI :, :].astype(F32).T
    line = jnp.sum((queries * grad).T, axis=0, keepdims=True)
    for row in range(ROWS):
        part = slice(row * HI, (row + 1) * HI)
        query_out[part, :] = grad[part] * weights[:HI, row : row + 1]
        weight_out[row : row + 1, :] = line[:, part]


def close_kernel(*refs):
    parts, divergence = refs[:SLOTS], refs[SLOTS]
    total = parts[0][...] + parts[1][...] + parts[2][...] + parts[3][...]
    divergence[0] = jnp.max(total) * (1.0 / ROW_TOTAL)


def pulled_from(value, axis, offset):
    size = lax.axis_size(axis)
    return lax.ppermute(value, axis, [((i + offset) % size, i) for i in range(size)])


def around(value, axis):
    return [value] + [pulled_from(value, axis, k) for k in range(1, lax.axis_size(axis))]


def local(
    main_query, main_key, index_query, index_key, head_weight, query_positions, key_positions
):
    z, x, y, core = (lax.axis_index(name) for name in ("z", "x", "y", "c"))
    place = jnp.stack([z, x, core, y]).astype(jnp.int32)
    kpos = key_positions.reshape(128, 128)
    where = [place, query_positions, kpos]

    row, near, far = call(
        prep_kernel,
        [place, head_weight],
        [((MESSAGE, H), BF16), ((WIDTH, HALF), BF16), ((WIDTH, HALF), BF16)],
        [((SHARD, DI), BF16)],
        name="prep",
        room=60 * 1024 * 1024,
        far=[
            main_query.transpose(0, 2, 1),
            index_query.reshape(ROWS * HI, DI),
            main_key.T,
            index_key,
        ],
        semaphores=14,
    )
    rows = {0: [row], 1: [pulled_from(row, "x", 1)], 3: [pulled_from(row, "x", -1)]}
    nears = {0: [near], 1: [pulled_from(near, "z", 1)], 3: [pulled_from(near, "z", -1)]}
    rows[2] = [pulled_from(rows[1][0][:SPLIT], "x", 1), pulled_from(rows[3][0][SPLIT:], "x", -1)]
    nears[2] = [pulled_from(nears[1][0][:CUT], "z", 1), pulled_from(nears[3][0][CUT:], "z", -1)]
    halves = {0: [[near], [far]]}
    for step in (1, 3, 2):
        halves[step] = [nears[step], [pulled_from(part, "c", 1) for part in nears[step]]]

    queries, packs, index_keys = {}, {}, {}
    for slot in NEAR:
        queries[slot], packs[slot] = turn(slot, rows[slot])
    terms = []
    carried = ()
    for phase in range(len(PHASES)):
        if phase == 2:
            queries[2], packs[2] = turn(2, rows[2], carried[1:])
        more, found, carried = work(phase, where, queries, packs, halves, carried)
        index_keys.update(found)
        terms += more
    packs = [packs[slot] for slot in ALL]
    logits, stats, message = carried
    messages = around(message, "x")
    ready = {step: mask(packs, index_keys[step], [message]) for step in (2, 1, 3, 0)}
    deltas, loss = call(
        target_kernel,
        messages + [stats, logits] + terms,
        [((GROUP, SLOTS * SHARD), F32), ((8, 128), F32)],
        [((GROUP, SLOTS * SHARD), F32)],
        name="target_pass",
        after=list(ready.values()),
        room=10 * 1024 * 1024,
    )

    masked = {}
    key_parts = {}
    sums = {}

    def gradient(step, after=()):
        near, far, masked[step] = key_gradient(step, deltas, loss, ready[step], packs, after)
        sums[step] = near + pulled_from(far, "c", 1)
        key_parts[step] = pulled_from(sums[step], "z", -step) if step else sums[step]

    gradient(2)
    gradient(1)
    gradient(3, [sums[2]])
    gradient(0, [sums[1]])
    grads = {}
    grads.update(zip((2, 1), query_gradient((2, 1), masked, index_keys, [sums[0], sums[3]])))
    received = [pulled_from(grads[k], "x", -k) for k in (1, 2)]
    grads.update(zip((3, 0), query_gradient((3, 0), masked, index_keys)))
    received.append(pulled_from(grads[3], "x", -3))
    blocks = call(
        key_block_kernel,
        [place] + [key_parts[step] for step in ALL],
        [((DI + 8, 128), F32)] * SLOTS,
        [((DI + 8, HALF), F32)],
        name="key_blocks",
        after=received[:2] + [grads[0]],
    )
    parts = [blocks[0]] + [pulled_from(blocks[k], "y", -k) for k in range(1, SLOTS)]
    grad_query, grad_weight = call(
        finish_kernel,
        [packs[0], grads[0]] + received,
        [((ROWS * HI, DI), F32), ((ROWS, HI), F32)],
        name="finish",
        after=[blocks[0]],
    )
    key_total, tile = call(
        seal_kernel,
        parts,
        [((DI, DI), F32), ((8, DI), F32)],
        name="seal",
        after=[grad_weight],
    )
    (divergence,) = call(close_kernel, around(tile, "x"), [((1,), F32)], name="close")
    return (
        divergence.reshape(()),
        grad_query.reshape(ROWS, HI, DI),
        grad_weight,
        key_total,
    )


def solution(mesh):
    fine = Mesh(mesh.devices.reshape(4, 4, 4, 2), ("z", "x", "y", "c"))
    rows = ("y", "c", "z", "x")
    keys = ("z", "x")
    return jax.shard_map(
        local,
        mesh=fine,
        in_specs=(
            P(rows, None, None),
            P(keys, None),
            P(rows, None, None),
            P(keys, None),
            P(rows, None),
            P(("y", "c")),
            P(),
        ),
        out_specs=(
            P(),
            P(rows, None, None),
            P(rows, None),
            P(("z", "x", "y", "c"), None),
        ),
        check_vma=False,
    )
```

```python
import jax
import jax.numpy as jnp
from jax import lax
from jax.experimental import pallas as pl
from jax.experimental.pallas import tpu as pltpu
from jax.sharding import Mesh, PartitionSpec as P

H = 128
DR = 64
DN = 128
HI = 64
DI = 128
DK = 576
ROWS = 4
SLOTS = 4
GROUP = ROWS * SLOTS
SHARD = 1024
HALF = SHARD // 2
DEEP = DK + GROUP
PACK = ROWS * HI + 16
SPLIT = 2 * DK + PACK
MESSAGE = 4 * DK + PACK
PACK_AT = 2 * DK
WIDTH = DK + DI
CUT = WIDTH // 2
ROW_TOTAL = 512
NEGATIVE = -1e30
LOG2E = 1.4426950408889634
SCALE2 = (DN + DR) ** (-0.5) * LOG2E
F32 = jnp.float32
BF16 = jnp.bfloat16
VMEM_LIMIT = 6 * 1024 * 1024
NEAR = (0, 1, 3)
ALL = (0, 1, 2, 3)
PHASES = (
    [(0, slot) for slot in NEAR],
    [(step, slot) for step in (1, 3) for slot in NEAR],
    [(step, 2) for step in NEAR],
    [(2, slot) for slot in ALL],
)


def call(kernel, inputs, outputs, scratch=(), name=None, flops=1, after=(), far=(), semaphores=0, room=VMEM_LIMIT):
    count = len(inputs) + len(far)

    def body(*refs):
        kernel(*refs[:count], *refs[count + len(after) :])

    return pl.pallas_call(
        body,
        in_specs=[
            pl.BlockSpec(memory_space=pltpu.SMEM if value.ndim == 1 else pltpu.VMEM)
            for value in inputs
        ]
        + [pl.BlockSpec(memory_space=pltpu.HBM)] * len(far)
        + [pl.BlockSpec(memory_space=pl.ANY)] * len(after),
        out_specs=[
            pl.BlockSpec(memory_space=pltpu.SMEM if len(shape) == 1 else pltpu.VMEM)
            for shape, _ in outputs
        ],
        out_shape=[jax.ShapeDtypeStruct(shape, dtype) for shape, dtype in outputs],
        scratch_shapes=[pltpu.VMEM(shape, dtype) for shape, dtype in scratch]
        + [pltpu.SemaphoreType.DMA((semaphores,))] * (semaphores > 0),
        compiler_params=pltpu.CompilerParams(vmem_limit_bytes=room),
        cost_estimate=pl.CostEstimate(flops=flops, bytes_accessed=1, transcendentals=0),
        name=name,
    )(*inputs, *far, *after)


def contract(a, b, dim_a, dim_b):
    return lax.dot_general(a, b, (((dim_a,), (dim_b,)), ((), ())), preferred_element_type=F32)


def largest(values):
    best = values[0]
    for value in values[1:]:
        best = jnp.maximum(best, value)
    return best


def row_position(place, qpos, slot, row):
    return qpos[place[0] * GROUP + lax.rem(place[1] + slot, SLOTS) * ROWS + row]


def key_positions_of(place, kpos, step):
    core = place[2]
    base = (lax.rem(place[0] + step, SLOTS) * SLOTS + place[1]) * 8
    pieces = [kpos[pl.ds(base + 2 * y + core, 1), :] for y in range(4)]
    pieces += [kpos[pl.ds(base + 2 * y + 1 - core, 1), :] for y in range(4)]
    return jnp.concatenate(pieces, axis=1)


def prep_kernel(place, weight, query, index_query, main_key, index_key, row, near, far, held, sems):
    core = place[2]
    copies = []

    def move(source, target):
        copies.append(pltpu.make_async_copy(source, target, sems.at[len(copies)]))
        copies[-1].start()

    move(index_key, held)
    for i in range(ROWS):
        move(query.at[i], row.at[pl.ds(i * DK + (PACK if i > 1 else 0), DK)])
    move(index_query, row.at[pl.ds(PACK_AT, ROWS * HI)])
    for y in range(4):
        for own, out in ((0, near), (1, far)):
            block = 2 * y + (core if own == 0 else 1 - core)
            start = pl.multiple_of(block * 128, 128)
            move(main_key.at[:, pl.ds(start, 128)], out.at[pl.ds(0, DK), pl.ds(y * 128, 128)])
    padded = jnp.concatenate([weight[...].astype(F32), jnp.zeros((ROWS, DI - HI), F32)], axis=1)
    padded = jnp.concatenate([padded, jnp.zeros((16 - ROWS, DI), F32)], axis=0)
    row[PACK_AT + ROWS * HI : SPLIT, :] = padded.astype(BF16)
    copies[0].wait()
    for y in range(4):
        for own, out in ((0, near), (1, far)):
            block = 2 * y + (core if own == 0 else 1 - core)
            start = pl.multiple_of(block * 128, 128)
            out[DK:, y * 128 : (y + 1) * 128] = held[pl.ds(start, 128), :].T
    for copy in copies[1:]:
        copy.wait()


def turn_kernel(slot, *refs):
    sources, (turned, pack) = refs[:-2], refs[-2:]
    pack[...] = sources[0][PACK_AT:SPLIT, :]
    lane = lax.broadcasted_iota(jnp.int32, (H, GROUP), 1)
    for row in range(ROWS):
        source, start = sources[0], row * DK
        if row > 1:
            source = sources[-1]
            start += PACK if len(sources) == 1 else PACK - SPLIT
        part = slice(row * H, (row + 1) * H)
        turned[part, :DK] = source[start : start + DK, :].T
        turned[part, DK:] = jnp.where(lane == slot * ROWS + row, 1.0, 0.0).astype(BF16)


def turn(slot, sources, after=()):
    return call(
        lambda *refs: turn_kernel(slot, *refs),
        sources,
        [((ROWS * H, DEEP), BF16), ((PACK, DI), BF16)],
        name="turn",
        after=after,
    )


def feature_rows(parts, start, stop):
    if len(parts) == 1:
        return [parts[0][start:stop, :]]
    pieces = []
    if start < CUT:
        pieces.append(parts[0][start : min(stop, CUT), :])
    if stop > CUT:
        pieces.append(parts[1][max(start, CUT) - CUT : stop - CUT, :])
    return pieces


FRESH = ((0,), (1, 3), (), (2,))


def work_kernel(units, final, slots, steps, fresh, place, qpos, kpos, *refs):
    refs = list(refs)
    queries = {slot: refs.pop(0) for slot in slots}
    packs = {slot: refs.pop(0) for slot in slots}
    halves = {}
    for step in steps:
        count = 2 if step == 2 else 1
        halves[step] = [[refs.pop(0) for _ in range(count)] for _ in range(2)]
    logits_before = stats_before = None
    if units is not PHASES[0]:
        logits_before, stats_before = refs.pop(0), refs.pop(0)
    terms = [refs.pop(0) for _ in units]
    index_out = {step: refs.pop(0) for step in fresh}
    logits, stat_out = refs.pop(0), refs.pop(0)
    message = refs.pop(0) if final else None
    keys, scores = refs
    if logits_before is None:
        logits[...] = jnp.zeros(logits.shape, F32)
        stats = {step: jnp.zeros((H, 128), F32) for step in ALL}
    else:
        logits[...] = logits_before[...]
        stats = {step: stats_before[step] for step in ALL}
    lane = lax.broadcasted_iota(jnp.int32, (H, 128), 1)
    weights = {slot: packs[slot][ROWS * HI :, :].astype(F32).T for slot in slots}
    staged = None
    waiting = []

    def finish(unit, pair):
        step, slot = units[unit]
        for row in range(2 * pair, 2 * pair + 2):
            values = terms[unit][row]
            best = jnp.max(values, axis=1, keepdims=True)
            part = jnp.exp2((values - best) * SCALE2)
            total = jnp.sum(part, axis=1, keepdims=True)
            terms[unit][row] = part
            index = slot * ROWS + row
            stats[step] = jnp.where(
                lane == index, best, jnp.where(lane == GROUP + index, total, stats[step])
            )

    for unit, (step, slot) in enumerate(units):
        if staged != step:
            staged = step
            for side in range(2):
                part = slice(side * HALF, (side + 1) * HALF)
                at = 0
                for piece in feature_rows(halves[step][side], 0, DK):
                    keys[at : at + piece.shape[0], part] = piece
                    at += piece.shape[0]
                if step in fresh:
                    (piece,) = feature_rows(halves[step][side], DK, WIDTH)
                    index_out[step][:, part] = piece
            position = key_positions_of(place, kpos, step)
            hidden = [
                jnp.where(position <= row_position(place, qpos, i // ROWS, i % ROWS), 0.0, NEGATIVE)
                for i in range(GROUP)
            ]
            keys[DK:, :] = jnp.concatenate(hidden, axis=0).astype(BF16)
        index_queries = packs[slot][: ROWS * HI, :]
        for side in range(2):
            (index_keys,) = feature_rows(halves[step][side], DK, WIDTH)
            scores[:, side * HALF : (side + 1) * HALF] = contract(index_queries, index_keys, 1, 0)
        for pair in range(2):
            part = slice(2 * pair * H, (2 * pair + 2) * H)
            product = contract(queries[slot][part, :], keys[...], 1, 0)
            terms[unit][2 * pair : 2 * pair + 2] = product.reshape(2, H, SHARD)
            if waiting:
                finish(*waiting.pop())
            waiting.append((unit, pair))
            for row in range(2 * pair, 2 * pair + 2):
                active = jnp.maximum(scores[row * HI : (row + 1) * HI, :], 0.0)
                line = jnp.sum(active * weights[slot][:HI, row : row + 1], axis=0, keepdims=True)
                visible = position <= row_position(place, qpos, slot, row)
                index = slot * ROWS + row
                logits[index : index + 1, step * SHARD : (step + 1) * SHARD] = jnp.where(
                    visible, line, NEGATIVE
                )
    finish(*waiting.pop())
    for step in ALL:
        stat_out[step] = stats[step]
    if not final:
        return
    best = largest([stats[step] for step in ALL])
    total = jnp.zeros((H, 128), F32)
    for step in ALL:
        factor = pltpu.roll(jnp.exp2((stats[step] - best) * SCALE2), GROUP, 1)
        total = total + stats[step] * jnp.where(
            (lane >= GROUP) & (lane < 2 * GROUP), factor, 0.0
        )
    both = jnp.where(lane < GROUP, best, total)
    message[: 2 * GROUP, :] = both.T[: 2 * GROUP, :]
    values = logits[...]
    best = jnp.max(values, axis=1, keepdims=True)
    total = jnp.sum(jnp.exp2((values - best) * LOG2E), axis=1, keepdims=True)
    message[2 * GROUP : 3 * GROUP, :] = jnp.broadcast_to(best, (GROUP, 128))
    message[3 * GROUP :, :] = jnp.broadcast_to(total, (GROUP, 128))


def work(phase, where, queries, packs, halves, carried, after=()):
    units = PHASES[phase]
    final = phase == len(PHASES) - 1
    slots = [slot for slot in ALL if any(unit[1] == slot for unit in units)]
    steps = [step for step in ALL if any(unit[0] == step for unit in units)]
    inputs = where + [queries[slot] for slot in slots] + [packs[slot] for slot in slots]
    for step in steps:
        inputs += halves[step][0] + halves[step][1]
    fresh = FRESH[phase]
    outputs = [((ROWS, H, SHARD), F32)] * len(units) + [((DI, SHARD), BF16)] * len(fresh)
    outputs += [((GROUP, SLOTS * SHARD), F32), ((SLOTS, H, 128), F32)]
    if final:
        outputs.append(((4 * GROUP, 128), F32))
    results = call(
        lambda *refs: work_kernel(units, final, slots, steps, fresh, *refs),
        inputs + list(carried),
        outputs,
        [((DEEP, SHARD), BF16), ((ROWS * HI, SHARD), F32)],
        name="work",
        room=3584 * 1024,
        flops=2 * len(units) * ROWS * SHARD * (H * DK + HI * DI),
        after=after,
    )
    end = len(units) + len(fresh)
    return results[: len(units)], dict(zip(fresh, results[len(units) : end])), results[end:]


def target_kernel(*refs):
    messages, stats, logits = refs[:4], refs[4], refs[5]
    terms, (deltas, loss, target) = refs[6:-3], refs[-3:]

    def field(index):
        return [
            jnp.concatenate(
                [
                    message[pl.ds(index * GROUP + (i - k) % SLOTS * ROWS, ROWS), :]
                    for i in range(SLOTS)
                ],
                axis=0,
            )
            for k, message in enumerate(messages)
        ]

    maxima, totals = field(0), field(1)
    best = largest(maxima)
    total = jnp.zeros((GROUP, 128), F32)
    for k in range(SLOTS):
        total = total + totals[k] * jnp.exp2((maxima[k] - best) * SCALE2)
    both = jnp.concatenate([best, 1.0 / (total * H), jnp.zeros((96, 128), F32)], axis=0).T
    factors = [
        jnp.exp2((stats[step][:, :GROUP] - both[:, :GROUP]) * SCALE2) * both[:, GROUP : 2 * GROUP]
        for step in ALL
    ]
    units = [unit for phase in PHASES for unit in phase]
    for part, (step, slot) in zip(terms, units):
        for row in range(ROWS):
            at = slot * ROWS + row
            total = jnp.zeros((8, SHARD), F32)
            for start in range(0, H, 8):
                lines = slice(start, start + 8)
                total = total + part[row, lines, :] * factors[step][lines, at : at + 1]
            target[at : at + 1, step * SHARD : (step + 1) * SHARD] = jnp.sum(
                total, axis=0, keepdims=True
            )
    maxima, totals = field(2), field(3)
    best = largest(maxima)
    total = jnp.zeros((GROUP, 128), F32)
    for k in range(SLOTS):
        total = total + totals[k] * jnp.exp2((maxima[k] - best) * LOG2E)
    best, total = best[:, :1], total[:, :1]
    norm = best + jnp.log(total)
    share = 1.0 / total
    lost = jnp.zeros((GROUP, 1), F32)
    for step in range(SLOTS):
        columns = slice(step * SHARD, (step + 1) * SHARD)
        wanted = target[:, columns]
        value = logits[:, columns]
        prob = jnp.exp2((value - best) * LOG2E) * share
        deltas[:, columns] = prob - wanted
        pieces = wanted * (jnp.log(jnp.maximum(wanted, 1e-37)) - (value - norm))
        lost = lost + jnp.sum(jnp.where(wanted > 0, pieces, 0.0), axis=1, keepdims=True)
    loss[...] = jnp.broadcast_to(jnp.sum(lost, axis=0, keepdims=True), (8, 128))


def mask_kernel(*refs):
    packs, (keys, out) = refs[:SLOTS], refs[SLOTS:]
    for slot in range(SLOTS):
        scores = contract(packs[slot][: ROWS * HI, :], keys[...], 1, 0)
        part = slice(slot * ROWS * HI, (slot + 1) * ROWS * HI)
        out[part, :] = jnp.where(scores > 0, 1.0, 0.0).astype(BF16)


def mask(packs, keys, after):
    return call(
        mask_kernel,
        packs + [keys],
        [((GROUP * HI, SHARD), BF16)],
        name="mask",
        flops=800000000,
        after=after,
    )[0]


def key_gradient_kernel(step, deltas, loss, active, *refs):
    packs, (key_near, key_far, highs, lows) = refs[:SLOTS], refs[SLOTS:]
    total = [jnp.zeros((2 * DI, HALF), F32), jnp.zeros((2 * DI, HALF), F32)]
    for slot in range(SLOTS):
        queries = packs[slot][: ROWS * HI, :]
        weights = packs[slot][ROWS * HI :, :].astype(F32).T
        product = jnp.concatenate(
            [
                queries[row * HI : (row + 1) * HI].astype(F32) * weights[:HI, row : row + 1]
                for row in range(ROWS)
            ],
            axis=0,
        )
        high = product.astype(BF16).astype(F32)
        both = jnp.concatenate([high.T, (product - high).T], axis=0).astype(BF16)
        part = slice(slot * ROWS * HI, (slot + 1) * ROWS * HI)
        for side in range(2):
            columns = slice(side * HALF, (side + 1) * HALF)
            for row in range(ROWS):
                at = slot * ROWS + row
                start = step * SHARD + side * HALF
                delta = deltas[at : at + 1, start : start + HALF]
                high = delta.astype(BF16)
                low = (delta - high.astype(F32)).astype(BF16)
                lines = slice(at * HI, (at + 1) * HI)
                highs[lines, columns] = active[lines, columns] * high
                lows[lines, columns] = active[lines, columns] * low
            wide = contract(both, highs[part, columns], 1, 0)
            narrow = contract(both[:DI], lows[part, columns], 1, 0)
            total[side] = total[side] + jnp.concatenate([wide[:DI] + narrow, wide[DI:]], axis=0)
    for side, out in enumerate((key_near, key_far)):
        out[:DI, :] = total[side][:DI] + total[side][DI:]
        out[DI:, :] = jnp.broadcast_to(loss[:, :1], (8, HALF))


def key_gradient(step, deltas, loss, active, packs, after=()):
    near, far, *masked = call(
        lambda *refs: key_gradient_kernel(step, *refs),
        [deltas, loss, active, *packs],
        [((DI + 8, HALF), F32)] * 2 + [((GROUP * HI, SHARD), BF16)] * 2,
        name="key_gradient",
        flops=1600000000,
        after=after,
    )
    return near, far, masked


def query_gradient_kernel(slots, *refs):
    masked, keys, outs = refs[: 2 * SLOTS], refs[2 * SLOTS : 3 * SLOTS], refs[3 * SLOTS :]
    for slot, out in zip(slots, outs):
        part = slice(slot * ROWS * HI, (slot + 1) * ROWS * HI)
        total = jnp.zeros((ROWS * HI, DI), F32)
        for step in ALL:
            for level in range(2):
                total = total + contract(masked[2 * step + level][part, :], keys[step][...], 1, 1)
        out[...] = total


def query_gradient(slots, masked, keys, after=()):
    return call(
        lambda *refs: query_gradient_kernel(slots, *refs),
        [level for step in ALL for level in masked[step]] + [keys[step] for step in ALL],
        [((ROWS * HI, DI), F32)] * len(slots),
        name="query_gradient",
        flops=len(slots) * 1300000000,
        after=after,
    )


def key_block_kernel(place, *refs):
    parts, outs = refs[:SLOTS], refs[SLOTS : 2 * SLOTS]
    total = refs[-1]
    total[...] = parts[0][...] + parts[1][...] + parts[2][...] + parts[3][...]
    for k in range(SLOTS):
        start = pl.multiple_of(lax.rem(place[3] + k, SLOTS) * 128, 128)
        outs[k][...] = total[:, pl.ds(start, 128)]


def seal_kernel(*refs):
    parts, (key_out, tile) = refs[:SLOTS], refs[SLOTS:]
    total = parts[0][...] + parts[1][...] + parts[2][...] + parts[3][...]
    key_out[...] = total[:DI].T
    tile[...] = total[DI:]


def finish_kernel(pack, *refs):
    parts, (query_out, weight_out) = refs[:SLOTS], refs[SLOTS:]
    grad = parts[0][...] + parts[1][...] + parts[2][...] + parts[3][...]
    queries = pack[: ROWS * HI, :].astype(F32)
    weights = pack[ROWS * HI :, :].astype(F32).T
    line = jnp.sum((queries * grad).T, axis=0, keepdims=True)
    for row in range(ROWS):
        part = slice(row * HI, (row + 1) * HI)
        query_out[part, :] = grad[part] * weights[:HI, row : row + 1]
        weight_out[row : row + 1, :] = line[:, part]


def close_kernel(*refs):
    parts, divergence = refs[:SLOTS], refs[SLOTS]
    total = parts[0][...] + parts[1][...] + parts[2][...] + parts[3][...]
    divergence[0] = jnp.max(total) * (1.0 / ROW_TOTAL)


def pulled_from(value, axis, offset):
    size = lax.axis_size(axis)
    return lax.ppermute(value, axis, [((i + offset) % size, i) for i in range(size)])


def around(value, axis):
    return [value] + [pulled_from(value, axis, k) for k in range(1, lax.axis_size(axis))]


def local(
    main_query, main_key, index_query, index_key, head_weight, query_positions, key_positions
):
    z, x, y, core = (lax.axis_index(name) for name in ("z", "x", "y", "c"))
    place = jnp.stack([z, x, core, y]).astype(jnp.int32)
    kpos = key_positions.reshape(128, 128)
    where = [place, query_positions, kpos]

    row, near, far = call(
        prep_kernel,
        [place, head_weight],
        [((MESSAGE, H), BF16), ((WIDTH, HALF), BF16), ((WIDTH, HALF), BF16)],
        [((SHARD, DI), BF16)],
        name="prep",
        room=60 * 1024 * 1024,
        far=[
            main_query.transpose(0, 2, 1),
            index_query.reshape(ROWS * HI, DI),
            main_key.T,
            index_key,
        ],
        semaphores=14,
    )
    rows = {0: [row], 1: [pulled_from(row, "x", 1)], 3: [pulled_from(row, "x", -1)]}
    nears = {0: [near], 1: [pulled_from(near, "z", 1)], 3: [pulled_from(near, "z", -1)]}
    rows[2] = [pulled_from(rows[1][0][:SPLIT], "x", 1), pulled_from(rows[3][0][SPLIT:], "x", -1)]
    nears[2] = [pulled_from(nears[1][0][:CUT], "z", 1), pulled_from(nears[3][0][CUT:], "z", -1)]
    halves = {0: [[near], [far]]}
    for step in (1, 3, 2):
        halves[step] = [nears[step], [pulled_from(part, "c", 1) for part in nears[step]]]

    queries, packs, index_keys = {}, {}, {}
    for slot in NEAR:
        queries[slot], packs[slot] = turn(slot, rows[slot])
    terms = []
    carried = ()
    for phase in range(len(PHASES)):
        if phase == 2:
            queries[2], packs[2] = turn(2, rows[2], carried[1:])
        more, found, carried = work(phase, where, queries, packs, halves, carried)
        index_keys.update(found)
        terms += more
    packs = [packs[slot] for slot in ALL]
    logits, stats, message = carried
    messages = around(message, "x")
    ready = {step: mask(packs, index_keys[step], [message]) for step in (2, 1, 3, 0)}
    deltas, loss = call(
        target_kernel,
        messages + [stats, logits] + terms,
        [((GROUP, SLOTS * SHARD), F32), ((8, 128), F32)],
        [((GROUP, SLOTS * SHARD), F32)],
        name="target_pass",
        after=list(ready.values()),
        room=10 * 1024 * 1024,
    )

    masked = {}
    key_parts = {}
    sums = {}

    def gradient(step, after=()):
        near, far, masked[step] = key_gradient(step, deltas, loss, ready[step], packs, after)
        sums[step] = near + pulled_from(far, "c", 1)
        key_parts[step] = pulled_from(sums[step], "z", -step) if step else sums[step]

    gradient(2)
    gradient(1)
    gradient(3, [sums[2]])
    gradient(0, [sums[1]])
    grads = {}
    grads.update(zip((2, 1), query_gradient((2, 1), masked, index_keys, [sums[0], sums[3]])))
    received = [pulled_from(grads[k], "x", -k) for k in (1, 2)]
    grads.update(zip((3, 0), query_gradient((3, 0), masked, index_keys)))
    received.append(pulled_from(grads[3], "x", -3))
    blocks = call(
        key_block_kernel,
        [place] + [key_parts[step] for step in ALL],
        [((DI + 8, 128), F32)] * SLOTS,
        [((DI + 8, HALF), F32)],
        name="key_blocks",
        after=received[:2] + [grads[0]],
    )
    parts = [blocks[0]] + [pulled_from(blocks[k], "y", -k) for k in range(1, SLOTS)]
    grad_query, grad_weight = call(
        finish_kernel,
        [packs[0], grads[0]] + received,
        [((ROWS * HI, DI), F32), ((ROWS, HI), F32)],
        name="finish",
        after=[blocks[0]],
    )
    key_total, tile = call(
        seal_kernel,
        parts,
        [((DI, DI), F32), ((8, DI), F32)],
        name="seal",
        after=[grad_weight],
    )
    (divergence,) = call(close_kernel, around(tile, "x"), [((1,), F32)], name="close")
    return (
        divergence.reshape(()),
        grad_query.reshape(ROWS, HI, DI),
        grad_weight,
        key_total,
    )


def solution(mesh):
    fine = Mesh(mesh.devices.reshape(4, 4, 4, 2), ("z", "x", "y", "c"))
    rows = ("y", "c", "z", "x")
    keys = ("z", "x")
    return jax.shard_map(
        local,
        mesh=fine,
        in_specs=(
            P(rows, None, None),
            P(keys, None),
            P(rows, None, None),
            P(keys, None),
            P(rows, None),
            P(("y", "c")),
            P(),
        ),
        out_specs=(
            P(),
            P(rows, None, None),
            P(rows, None),
            P(("z", "x", "y", "c"), None),
        ),
        check_vma=False,
    )
```
